32 devices in a mesh: dp: 8 (over z, y), tensor: 4 (over x, core).
Axes of the slice: x: 2, y: 2, z: 4, core: 2. Of those that a mesh axis runs over, the one named last changes fastest.
Arguments:
- gradient: bfloat16 [8, 4608, 1024], P('dp', None, 'tensor'), may hold values from -6 to 6
- error_buffer: float32 [8, 4608, 1024], P('dp', None, 'tensor'), may hold values from -4 to 4
- q_given: float32 [1024, 32], P('tensor'), may hold values from -6 to 6
Outputs:
- new_error: float32 [8, 4608, 1024], P('dp', None, 'tensor')
- p_hat: float32 [4608, 32], replicated
- q_new: float32 [1024, 32], P('tensor')
The draws below stay inside these ranges and needn't reach their ends.
All inputs are finite; a program needn't handle non-finite values.
Results may differ from the reference program's by a relative error of at most 0.0003.
Values sent between devices are 32-bit elements; how exact they have to be, the bound alone decides.
No kernel may reach another device: no remote copies, remote signals or barrier semaphores. Data moves between devices by JAX's collectives and lax.ppermute only.
A program may use at most 64 MiB of HBM per device.

```python
import jax
import jax.numpy as jnp
from jax import lax

D = 4608
RANK = 32
COLS = 1024
REPLICAS = 8


def block_scale(stream_key, extent, cuts, low, high):
    loudness, own = 1.0, jax.random.fold_in(stream_key, 6)
    for position, blocks in cuts:
        heights = jnp.exp(jax.random.uniform(jax.random.fold_in(own, position), (blocks,), jnp.float32, low / len(cuts), high / len(cuts)))
        loudness = loudness * jnp.repeat(heights, extent[position] // blocks).reshape([-1 if axis == position else 1 for axis in range(len(extent))])
    return loudness


def normal_values(key, dims, scale, limit, cuts=(), dtype=jnp.bfloat16):
    entries = scale * jax.random.normal(key, dims, jnp.float32)
    if cuts:
        entries = entries * block_scale(key, dims, cuts, -0.22, 0.18)
    return jnp.clip(entries, -limit, limit).astype(dtype)


def setup_inputs(seed: int = 0) -> dict:
    seeds = jax.random.split(jax.random.key(seed), 4)
    return {
        "gradient": normal_values(seeds[0], (REPLICAS, D, COLS), 1.0, 6.0, ((0, 8), (2, 4))),
        "error_buffer": normal_values(seeds[1], (REPLICAS, D, COLS), 0.5, 4.0, ((0, 8), (2, 4)), jnp.float32),
        "q_given": normal_values(seeds[2], (COLS, RANK), 1.0, 6.0, ((0, 4),), jnp.float32),
    }


def merge_one(grad_one, error_one):
    return grad_one.astype(jnp.float32) + error_one

def reference(gradient, error_buffer, q_given):
    highest = lax.Precision.HIGHEST

    def add_p(total, pair):
        merged = merge_one(pair[0], pair[1])
        return (total + jnp.dot(merged.astype(jnp.float32), q_given.astype(jnp.float32), precision=highest, preferred_element_type=jnp.float32), None)
    p_sum, _ = lax.scan(add_p, jnp.zeros((D, RANK), jnp.float32), (gradient, error_buffer))
    gram = jnp.dot(p_sum.T.astype(jnp.float32), p_sum.astype(jnp.float32), precision=highest, preferred_element_type=jnp.float32)
    chol = jnp.linalg.cholesky(gram)
    p_hat = lax.linalg.triangular_solve(chol, p_sum, left_side=False, lower=True, transpose_a=True)

    def add_q(total, pair):
        merged = merge_one(pair[0], pair[1])
        return (total + jnp.dot(merged.T.astype(jnp.float32), p_hat.astype(jnp.float32), precision=highest, preferred_element_type=jnp.float32), None)
    q_sum, _ = lax.scan(add_q, jnp.zeros((COLS, RANK), jnp.float32), (gradient, error_buffer))
    q_new = q_sum / REPLICAS
    approx = jnp.dot(p_hat.astype(jnp.float32), q_new.T.astype(jnp.float32), precision=highest, preferred_element_type=jnp.float32)

    def one_error(pair):
        return merge_one(pair[0], pair[1]) - approx
    new_error = lax.map(one_error, (gradient, error_buffer))
    return (new_error, p_hat, q_new)
```

```python
import functools

import jax
import jax.numpy as jnp
from jax import lax
from jax.experimental import pallas as pl
from jax.experimental.pallas import tpu as pltpu
from jax.sharding import PartitionSpec as P

F32, BF16 = jnp.float32, jnp.bfloat16
VMEM = pl.BlockSpec(memory_space=pltpu.VMEM)
ANY = pl.BlockSpec(memory_space=pl.ANY)
AXES = ("dp", "tensor")
LIMIT = 24 * 2**20


def split(x, terms):
    out = []
    for _ in range(terms):
        t = x.astype(BF16)
        out.append(t)
        x = x - t.astype(F32)
    return out


def dot(a, b, contract):
    return lax.dot_general(a, b, ((contract[:1], contract[1:]), ((), ())), preferred_element_type=F32)


def fold(x, rank):
    return functools.reduce(jnp.add, [x[i : i + rank] for i in range(0, x.shape[0], rank)])


def halving_bit(dp, chip, core):
    return chip & 1


def quarters(dp, tensor):
    core, chip = tensor & 1, tensor >> 1
    mine, theirs = halving_bit(dp, chip, core), halving_bit(dp, chip, 1 - core)
    return 2 * core + mine, 2 * core + 1 - mine, 2 * (1 - core) + theirs, 2 * (1 - core) + 1 - theirs


def left_kernel(q_ref, g_hbm, e_hbm, m_ref, mh_ref, ml_ref, send_ref, keep_ref, g_buf, sems, *, chunk):
    own, other, partner_own, partner_other = quarters(lax.axis_index("dp"), lax.axis_index("tensor"))
    rank = q_ref.shape[0]
    quarter = send_ref.shape[2]
    places = ((partner_other, send_ref, 0), (partner_own, send_ref, 1), (other, keep_ref, 0), (own, keep_ref, 1))
    steps = [(pl.multiple_of(index * quarter + at, chunk), out, slot, at) for index, out, slot in places for at in range(0, quarter, chunk)]
    copies = []
    for n, (row, _, _, _) in enumerate(steps):
        rows = pl.ds(row, chunk)
        pair = (
            pltpu.make_async_copy(g_hbm.at[rows], g_buf.at[pl.ds(n * chunk, chunk)], sems.at[n, 0]),
            pltpu.make_async_copy(e_hbm.at[rows], m_ref.at[rows], sems.at[n, 1]),
        )
        for copy in pair:
            copy.start()
        copies.append(pair)
    q = jnp.concatenate(split(q_ref[...], 3), axis=0)
    for n, (row, out, slot, at) in enumerate(steps):
        for copy in copies[n]:
            copy.wait()
        rows = pl.ds(row, chunk)
        m = m_ref[rows] + g_buf[n * chunk : (n + 1) * chunk].astype(F32)
        m_ref[rows] = m
        mh, ml = split(m, 2)
        mh_ref[rows] = mh
        ml_ref[rows] = ml
        out[slot, :, at : at + chunk] = fold(dot(q, mh, (1, 1)) + dot(q, ml, (1, 1)), rank)


def right_kernel(p0, p1, p2, p3, mh_ref, ml_ref, t_ref, gram_ref):
    places = quarters(lax.axis_index("dp"), lax.axis_index("tensor"))
    rank, quarter = p0.shape
    t = gram = None
    for ref, index in zip((p0, p1, p2, p3), places, strict=True):
        rows = pl.ds(pl.multiple_of(index * quarter, quarter), quarter)
        p = jnp.concatenate(split(ref[...], 3), axis=0)
        part = dot(p, mh_ref[rows], (1, 0)) + dot(p, ml_ref[rows], (1, 0))
        square = dot(p, p, (1, 1))
        t = part if t is None else t + part
        gram = square if gram is None else gram + square
    t_ref[...] = fold(t, rank)
    gram = fold(gram, rank)
    gram_ref[...] = gram[:, :rank] + gram[:, rank : 2 * rank] + gram[:, 2 * rank :]


def factor_kernel(gram_ref, inv_ref):
    rank = gram_ref.shape[0]
    row = lax.broadcasted_iota(jnp.int32, (rank, 128), 0)
    lane = lax.broadcasted_iota(jnp.int32, (rank, 128), 1)
    eye = (lane == row + rank).astype(F32)
    a = jnp.concatenate([gram_ref[...], eye[:, rank:]], axis=1)
    pivots = jnp.zeros((rank, 1), F32)
    for k in range(rank):
        line, column = a[k : k + 1, :], a[:, k : k + 1]
        pivot = a[k : k + 1, k : k + 1]
        pivots = jnp.where(row[:, :1] == k, pivot, pivots)
        if k < rank - 1:
            a = a - jnp.where(row[:, :1] > k, column, 0.0) * (line / pivot)
    inv_ref[...] = a[:, rank : 2 * rank] / jnp.sqrt(pivots)


def hat_kernel(inv_ref, p0, p1, p2, p3, hat_ref, rows_ref):
    places = quarters(lax.axis_index("dp"), lax.axis_index("tensor"))
    rank, quarter = p0.shape
    a, b, c = split(inv_ref[...], 3)
    left = jnp.concatenate([a, a, b, a, b, c], axis=1)
    for ref, index in zip((p0, p1, p2, p3), places, strict=True):
        start = pl.multiple_of(index * quarter, quarter)
        u, v, w = split(ref[...], 3)
        hat = dot(left, jnp.concatenate([u, v, u, w, v, u], axis=0), (1, 0))
        hat_ref[:, pl.ds(start, quarter)] = hat
        u, v = split(hat, 2)
        rows_ref[pl.ds(start, quarter), :] = jnp.concatenate([u, v, u, v], axis=0).T


def error_kernel(t0_ref, t1_ref, inv_ref, rows_ref, m_ref, out_ref, q_ref, terms, *, replicas):
    block = out_ref.shape[0]
    step = pl.program_id(0)

    @pl.when(step == 0)
    def _():
        q = jnp.dot(inv_ref[...], t0_ref[...] + t1_ref[...], precision=lax.Precision.HIGHEST, preferred_element_type=F32) / replicas
        q_ref[...] = q
        u, v = split(q, 2)
        terms[...] = jnp.concatenate([u, u, v, v], axis=0)

    rows = pl.ds(pl.multiple_of(step * block, block), block)
    out_ref[...] = m_ref[rows, :] - dot(rows_ref[rows, :], terms[...], (1, 0))


def shards(gradient, error_buffer, q_given):
    replicas, tensors = lax.axis_size("dp"), lax.axis_size("tensor")
    depth, columns = gradient.shape[1:]
    rank = q_given.shape[1]
    quarter = depth // 4
    chunk = next(n for n in (384, 256, 128) if quarter % n == 0)
    steps = depth // chunk
    params = functools.partial(pltpu.CompilerParams, vmem_limit_bytes=LIMIT)

    m, mh, ml, send, keep = pl.pallas_call(
        functools.partial(left_kernel, chunk=chunk),
        out_shape=(
            pltpu.VMEM((depth, columns), F32),
            pltpu.VMEM((depth, columns), BF16),
            pltpu.VMEM((depth, columns), BF16),
            pltpu.VMEM((2, rank, quarter), F32),
            pltpu.VMEM((2, rank, quarter), F32),
        ),
        in_specs=[VMEM, ANY, ANY],
        out_specs=(VMEM,) * 5,
        scratch_shapes=[pltpu.VMEM((depth, columns), BF16), pltpu.SemaphoreType.DMA((steps, 2))],
        compiler_params=params(),
        cost_estimate=pl.CostEstimate(flops=12 * depth * columns * rank, bytes_accessed=6 * depth * columns, transcendentals=0),
        name="left_products",
    )(q_given.T, gradient[0], error_buffer[0])

    def swap(x, bit):
        return lax.ppermute(x, AXES, [(i, i ^ bit) for i in range(replicas * tensors)])

    got = swap(send, 1)
    first = 2
    acc = keep[1] + got[1] + swap(keep[0] + got[0], first)
    bit = 2 * first
    while bit < replicas * tensors:
        acc = acc + swap(acc, bit)
        bit *= 2
    p_own = acc
    p_other = swap(p_own, first)
    p_partner_own = swap(p_own, 1)
    p_partner_other = swap(p_other, 1)
    ps = (p_own, p_other, p_partner_own, p_partner_other)

    t, gram = pl.pallas_call(
        right_kernel,
        out_shape=(pltpu.VMEM((rank, columns), F32), pltpu.VMEM((rank, rank), F32)),
        in_specs=[VMEM] * 6,
        out_specs=(VMEM, VMEM),
        compiler_params=params(),
        cost_estimate=pl.CostEstimate(flops=12 * depth * columns * rank, bytes_accessed=4 * depth * columns, transcendentals=0),
        name="right_products",
    )(*ps, mh, ml)

    inverse = pl.pallas_call(
        factor_kernel,
        out_shape=pltpu.VMEM((rank, rank), F32),
        in_specs=[VMEM],
        out_specs=VMEM,
        compiler_params=params(),
        cost_estimate=pl.CostEstimate(flops=rank**3, bytes_accessed=4 * rank * rank, transcendentals=0),
        name="factor",
    )(gram)

    hat, hat_rows = pl.pallas_call(
        hat_kernel,
        out_shape=(jax.ShapeDtypeStruct((rank, depth), F32), pltpu.VMEM((depth, 4 * rank), BF16)),
        in_specs=[VMEM] * 5,
        out_specs=(VMEM, VMEM),
        compiler_params=params(),
        cost_estimate=pl.CostEstimate(flops=12 * depth * rank * rank, bytes_accessed=8 * depth * rank, transcendentals=0),
        name="left_factor",
    )(inverse, *ps)

    bit = tensors
    while 2 * bit < replicas * tensors:
        t = t + swap(t, bit)
        bit *= 2
    last = swap(t, bit)

    block = next(n for n in (512, 256, 128) if depth % n == 0)
    error, q_new = pl.pallas_call(
        functools.partial(error_kernel, replicas=replicas),
        grid=(depth // block,),
        out_shape=(jax.ShapeDtypeStruct((depth, columns), F32), jax.ShapeDtypeStruct((rank, columns), F32)),
        in_specs=[VMEM] * 5,
        out_specs=(pl.BlockSpec((block, columns), lambda i: (i, 0)), VMEM),
        scratch_shapes=[pltpu.VMEM((4 * rank, columns), BF16)],
        compiler_params=params(),
        cost_estimate=pl.CostEstimate(flops=2 * 4 * depth * rank * columns, bytes_accessed=8 * depth * columns, transcendentals=0),
        name="new_error",
    )(t, last, inverse, hat_rows, m)
    return (error[None], hat.T, q_new.T)


def solution(mesh):
    placed = (P("dp", None, "tensor"), P("dp", None, "tensor"), P("tensor", None))
    return jax.shard_map(
        shards,
        mesh=mesh,
        in_specs=placed,
        out_specs=(P("dp", None, "tensor"), P(), P("tensor", None)),
        check_vma=False,
    )
```

```python
import functools

import jax
import jax.numpy as jnp
from jax import lax
from jax.experimental import pallas as pl
from jax.experimental.pallas import tpu as pltpu
from jax.sharding import PartitionSpec as P

F32, BF16 = jnp.float32, jnp.bfloat16
VMEM = pl.BlockSpec(memory_space=pltpu.VMEM)
HBM = pl.BlockSpec(memory_space=pltpu.HBM)
AXES = ("dp", "tensor")
LIMIT = 24 * 2**20


def split(x, terms):
    out = []
    for _ in range(terms):
        t = x.astype(BF16)
        out.append(t)
        x = x - t.astype(F32)
    return out


def stack(terms):
    return jnp.concatenate(terms, axis=0)


def dot(a, b, contract):
    return lax.dot_general(a, b, ((contract[:1], contract[1:]), ((), ())), preferred_element_type=F32)


def fold(x, rank):
    return functools.reduce(jnp.add, [x[i : i + rank] for i in range(0, x.shape[0], rank)])


def walks(devices):
    bits = []
    bit = 2
    while bit < devices:
        bits.append(bit)
        bit *= 2
    half = len(bits) // 2
    return bits, bits[half:] + bits[:half][::-1]


def sides(devices):
    place = lax.axis_index("dp") * lax.axis_size("tensor") + lax.axis_index("tensor")
    first, second = (walk[0].bit_length() - 1 for walk in walks(devices))
    core = place & 1
    own = [(place >> first) & 1, (place >> second) & 1]
    mine = jnp.where(core == 0, own[0], own[1])
    theirs = jnp.where(core == 0, own[1], own[0])
    return (core, mine), (1 - core, theirs)


def left_kernel(q_hbm, g_hbm, e_hbm, m_ref, mh_ref, ml_ref, send_a, send_b, keep_a, keep_b, q_buf, g_buf, q_sem, sems, *, chunk, devices):
    mine, theirs = sides(devices)
    rank, quarter = q_buf.shape[0], send_a.shape[2]
    half = rank // 2
    q_copy = pltpu.make_async_copy(q_hbm, q_buf, q_sem)
    q_copy.start()
    places = ((theirs, 0, send_a), (theirs, 1, send_b), (mine, 0, keep_a), (mine, 1, keep_b))
    steps = [(side, pl.multiple_of((2 * side[0] + k) * quarter + at, chunk), out, at) for side, k, out in places for at in range(0, quarter, chunk)]
    copies = []
    for n, (_, row, _, _) in enumerate(steps):
        rows = pl.ds(row, chunk)
        pair = (
            pltpu.make_async_copy(g_hbm.at[rows], g_buf.at[pl.ds(n * chunk, chunk)], sems.at[n, 0]),
            pltpu.make_async_copy(e_hbm.at[rows], m_ref.at[rows], sems.at[n, 1]),
        )
        for copy in pair:
            copy.start()
        copies.append(pair)
    q_copy.wait()
    factors = {}
    for side in (theirs, mine):
        ordered = stack([q_buf[pl.ds(pl.multiple_of(at * half, half), half), :] for at in (1 - side[1], side[1])])
        q = stack(split(ordered, 3))
        factors[id(side)] = jnp.concatenate([q, q], axis=1)
    for n, (side, row, out, at) in enumerate(steps):
        for copy in copies[n]:
            copy.wait()
        rows = pl.ds(row, chunk)
        m = m_ref[rows] + g_buf[n * chunk : (n + 1) * chunk].astype(F32)
        m_ref[rows] = m
        mh, ml = split(m, 2)
        mh_ref[rows] = mh
        ml_ref[rows] = ml
        p = fold(dot(jnp.concatenate([mh, ml], axis=1), factors[id(side)], (1, 1)).T, rank)
        out[0, :, at : at + chunk] = p[:half]
        out[1, :, at : at + chunk] = p[half:]


def whole(own, other, bit):
    a, b = own[...], other[...]
    return stack([jnp.where(bit == 0, a, b), jnp.where(bit == 0, b, a)])


def square(p, rank):
    g = fold(dot(p, p, (1, 1)), rank)
    return g[:, :rank] + g[:, rank : 2 * rank] + g[:, 2 * rank :]


def right_kernel(a0, a1, b0, b1, mh_ref, ml_ref, *refs, mine, devices):
    core, bit = sides(devices)[0 if mine else 1]
    quarter = a0.shape[1]
    rank = 2 * a0.shape[0]
    t = gram = None
    for k, pair in enumerate(((a0, a1), (b0, b1))):
        rows = pl.ds(pl.multiple_of((2 * core + k) * quarter, quarter), quarter)
        p = stack(split(whole(*pair, bit), 3))
        part = dot(p, mh_ref[rows], (1, 0)) + dot(p, ml_ref[rows], (1, 0))
        t = part if t is None else t + part
        if mine:
            g = square(p, rank)
            gram = g if gram is None else gram + g
    if mine:
        t_ref, gram_ref = refs
        t_ref[...] = fold(t, rank)
        gram_ref[...] = gram
    else:
        before, t_ref = refs
        t_ref[...] = before[...] + fold(t, rank)


def eliminate(a, pivots):
    rank = a.shape[0]
    row = lax.broadcasted_iota(jnp.int32, (rank, 1), 0)
    for k in pivots:
        line = a[k : k + 1, :] / a[k : k + 1, k : k + 1]
        a = a - jnp.where(row > k, a[:, k : k + 1], 0.0) * line
    return a


def factor_kernel(gram_ref, a0, a1, b0, b1, state_ref, *, devices):
    _, bit = sides(devices)[1]
    rank = gram_ref.shape[0]
    gram = gram_ref[...]
    for pair in ((a0, a1), (b0, b1)):
        gram = gram + square(stack(split(whole(*pair, bit), 3)), rank)
    row = lax.broadcasted_iota(jnp.int32, (rank, 128), 0)
    lane = lax.broadcasted_iota(jnp.int32, (rank, 128), 1)
    eye = (lane == row + rank).astype(F32)
    state_ref[...] = eliminate(jnp.concatenate([gram, eye[:, rank:]], axis=1), range(rank // 2))


def inverse_kernel(state_ref, inv_ref):
    rank = state_ref.shape[0]
    a = eliminate(state_ref[...], range(rank // 2, rank - 1))
    row = lax.broadcasted_iota(jnp.int32, a.shape, 0)
    lane = lax.broadcasted_iota(jnp.int32, a.shape, 1)
    pivots = jnp.sum(jnp.where(row == lane, a, 0.0), axis=1, keepdims=True)
    inv_ref[...] = a[:, rank : 2 * rank] / jnp.sqrt(pivots)


def hat_kernel(inv_ref, *refs, devices):
    pieces, (hat_ref, rows_ref) = refs[:8], refs[8:]
    quarter = pieces[0].shape[1]
    a, b, c = split(inv_ref[...], 3)
    left = jnp.concatenate([a, a, b, a, b, c], axis=1)
    for n, (core, bit) in enumerate(sides(devices)):
        for k in range(2):
            start = pl.multiple_of((2 * core + k) * quarter, quarter)
            u, v, w = split(whole(*pieces[4 * n + 2 * k : 4 * n + 2 * k + 2], bit), 3)
            hat = dot(left, stack([u, v, u, w, v, u]), (1, 0))
            hat_ref[:, pl.ds(start, quarter)] = hat
            u, v = split(hat, 2)
            rows_ref[pl.ds(start, quarter), :] = stack([u, v, u, v]).T


def error_kernel(t0_ref, t1_ref, inv_ref, rows_ref, m_ref, out_hbm, q_ref, buf, sems, *, replicas, block):
    q = jnp.dot(inv_ref[...], t0_ref[...] + t1_ref[...], precision=lax.Precision.HIGHEST, preferred_element_type=F32) / replicas
    q_ref[...] = q
    u, v = split(q, 2)
    terms = stack([u, u, v, v])
    copies = []
    for n in range(buf.shape[0] // block):
        rows = slice(n * block, (n + 1) * block)
        buf[rows] = m_ref[rows] - dot(rows_ref[rows], terms, (1, 0))
        copy = pltpu.make_async_copy(buf.at[pl.ds(n * block, block)], out_hbm.at[pl.ds(n * block, block)], sems.at[n])
        copy.start()
        copies.append(copy)
    for copy in copies:
        copy.wait()


def shards(gradient, error_buffer, q_given):
    replicas, tensors = lax.axis_size("dp"), lax.axis_size("tensor")
    devices = replicas * tensors
    depth, columns = gradient.shape[1:]
    rank = q_given.shape[1]
    half, quarter = rank // 2, depth // 4
    chunk = next(n for n in (384, 256, 128) if quarter % n == 0)
    steps = depth // chunk

    def call(kernel, name, flops, **kw):
        return pl.pallas_call(
            kernel,
            name=name,
            compiler_params=pltpu.CompilerParams(vmem_limit_bytes=LIMIT),
            cost_estimate=pl.CostEstimate(flops=flops, bytes_accessed=0, transcendentals=0),
            **kw,
        )

    in_hbm = [pltpu.with_memory_space_constraint(x, pltpu.HBM) for x in (q_given.T, gradient[0], error_buffer[0])]
    piece = pltpu.VMEM((2, half, quarter), F32)
    m, mh, ml, *partial = call(
        functools.partial(left_kernel, chunk=chunk, devices=devices),
        "left_products",
        12 * depth * columns * rank,
        out_shape=(pltpu.VMEM((depth, columns), F32), pltpu.VMEM((depth, columns), BF16), pltpu.VMEM((depth, columns), BF16)) + (piece,) * 4,
        in_specs=[HBM] * 3,
        out_specs=(VMEM,) * 7,
        scratch_shapes=[
            pltpu.VMEM((rank, columns), F32),
            pltpu.VMEM((depth, columns), BF16),
            pltpu.SemaphoreType.DMA(()),
            pltpu.SemaphoreType.DMA((steps, 2)),
        ],
    )(*in_hbm)

    def swap(x, bit, bit1=None):
        choice = (bit, bit if bit1 is None else bit1)
        return lax.ppermute(x, AXES, [(i, i ^ choice[i & 1]) for i in range(devices)])

    walk = list(zip(*walks(devices), strict=True))
    sums = [swap(send, 1) for send in partial[:2]]
    sums = [keep + got for keep, got in zip(partial[2:], sums, strict=True)]
    arrived = [swap(x[0], *walk[0]) for x in sums]
    sums = [x[1] + got for x, got in zip(sums, arrived, strict=True)]
    for bits in walk[1:]:
        arrived = [swap(x, *bits) for x in sums]
        sums = [x + got for x, got in zip(sums, arrived, strict=True)]
    others = [swap(x, *walk[0]) for x in sums]
    mine = (sums[0], others[0], sums[1], others[1])
    theirs = tuple(swap(x, 1) for x in mine)

    wide = (pltpu.VMEM((rank, columns), F32), pltpu.VMEM((rank, rank), F32))
    t, gram = call(
        functools.partial(right_kernel, mine=True, devices=devices),
        "right_products_own",
        6 * depth * columns * rank,
        out_shape=wide,
        in_specs=[VMEM] * 6,
        out_specs=(VMEM, VMEM),
    )(*mine, mh, ml)
    t = call(
        functools.partial(right_kernel, mine=False, devices=devices),
        "right_products_other",
        6 * depth * columns * rank,
        out_shape=wide[0],
        in_specs=[VMEM] * 7,
        out_specs=VMEM,
    )(*theirs, mh, ml, t)

    state = call(
        functools.partial(factor_kernel, devices=devices),
        "factor_first_half",
        6 * depth * columns * rank,
        out_shape=pltpu.VMEM((rank, 128), F32),
        in_specs=[VMEM] * 5,
        out_specs=VMEM,
    )(gram, *theirs)
    inverse = call(
        inverse_kernel,
        "factor_second_half",
        6 * depth * columns * rank,
        out_shape=pltpu.VMEM((rank, rank), F32),
        in_specs=[VMEM],
        out_specs=VMEM,
    )(state)
    hat, hat_rows = call(
        functools.partial(hat_kernel, devices=devices),
        "left_factor",
        6 * depth * columns * rank,
        out_shape=(jax.ShapeDtypeStruct((rank, depth), F32), pltpu.VMEM((depth, 4 * rank), BF16)),
        in_specs=[VMEM] * 9,
        out_specs=(VMEM, VMEM),
    )(inverse, *mine, *theirs)

    bits = [bit for bit in walks(devices)[0] if bit >= tensors]
    work = [state, inverse]
    got = swap(t, bits[0])
    for n, bit in enumerate(bits[1:]):
        t = t + got
        if n < len(work):
            t, _ = lax.optimization_barrier((t, work[n]))
        got = swap(t, bit)

    block = next(n for n in (512, 256, 128) if depth % n == 0)
    error, q_new = call(
        functools.partial(error_kernel, replicas=replicas, block=block),
        "new_error",
        8 * depth * rank * columns,
        out_shape=(pltpu.HBM((depth, columns), F32), jax.ShapeDtypeStruct((rank, columns), F32)),
        in_specs=[VMEM] * 5,
        out_specs=(HBM, VMEM),
        scratch_shapes=[pltpu.VMEM((depth, columns), F32), pltpu.SemaphoreType.DMA((depth // block,))],
    )(t, got, inverse, hat_rows, m)
    return (error[None], hat.T, q_new.T)


def solution(mesh):
    placed = (P("dp", None, "tensor"), P("dp", None, "tensor"), P("tensor", None))
    return jax.shard_map(
        shards,
        mesh=mesh,
        in_specs=placed,
        out_specs=(P("dp", None, "tensor"), P(), P("tensor", None)),
        check_vma=False,
    )
```

```python
import functools

import jax
import jax.numpy as jnp
from jax import lax
from jax.experimental import pallas as pl
from jax.experimental.pallas import tpu as pltpu
from jax.sharding import PartitionSpec as P

F32, BF16 = jnp.float32, jnp.bfloat16
VMEM = pl.BlockSpec(memory_space=pltpu.VMEM)
HBM = pl.BlockSpec(memory_space=pltpu.HBM)
AXES = ("dp", "tensor")
LIMIT = 12 * 2**20


def split(x, terms):
    out = []
    for _ in range(terms):
        t = x.astype(BF16)
        out.append(t)
        x = x - t.astype(F32)
    return out


def stack(terms):
    return jnp.concatenate(terms, axis=0)


def dot(a, b, contract):
    return lax.dot_general(a, b, ((contract[:1], contract[1:]), ((), ())), preferred_element_type=F32)


def fold(x, rank):
    return functools.reduce(jnp.add, [x[i : i + rank] for i in range(0, x.shape[0], rank)])


def six_left(x):
    a, b, c = split(x, 3)
    return jnp.concatenate([a, a, b, a, b, c], axis=1)


def six_right(x):
    u, v, w = split(x, 3)
    return stack([u, v, u, w, v, u])


def walks(devices):
    bits = []
    bit = 2
    while bit < devices:
        bits.append(bit)
        bit *= 2
    half = len(bits) // 2
    return bits, bits[half:] + bits[:half][::-1]


def sides(devices):
    place = lax.axis_index("dp") * lax.axis_size("tensor") + lax.axis_index("tensor")
    first, second = (walk[0].bit_length() - 1 for walk in walks(devices))
    core = place & 1
    own = [(place >> first) & 1, (place >> second) & 1]
    mine = jnp.where(core == 0, own[0], own[1])
    theirs = jnp.where(core == 0, own[1], own[0])
    return (core, mine), (1 - core, theirs)


def order(devices):
    mine, theirs = sides(devices)
    return tuple(2 * side[0] + k for k in range(2) for side in (theirs, mine))


def copies_of(quarter, rows, g_hbm, e_hbm, g_to, e_to, sems):
    at = pl.ds(pl.multiple_of(quarter * rows, rows), rows)
    return (
        pltpu.make_async_copy(g_hbm.at[at], g_to, sems.at[0]),
        pltpu.make_async_copy(e_hbm.at[at], e_to, sems.at[1]),
    )


def products(q, m, mh_ref, ml_ref, at, outs):
    rows = m.shape[0]
    mh, ml = split(m, 2)
    mh_ref[at : at + rows] = mh
    ml_ref[at : at + rows] = ml
    p = fold(dot(q, mh, (1, 1)) + dot(q, ml, (1, 1)), outs[0].shape[0])
    width = outs[0].shape[1]
    for n, out in enumerate(outs):
        out[...] = p[:, n * width : (n + 1) * width]


def start(pairs):
    for pair in pairs:
        for copy in pair:
            copy.start()


def wait(pairs):
    for pair in pairs:
        for copy in pair:
            copy.wait()


def left_kernel(q_hbm, g_hbm, e_hbm, m_ref, mh_ref, ml_ref, e_ref, g_ref, send, keep, q_buf, g_buf, q_sem, sems, *, devices):
    rows = send.shape[2]
    q_copy = pltpu.make_async_copy(q_hbm, q_buf, q_sem)
    q_copy.start()
    copies = []
    for n, quarter in enumerate(order(devices)):
        at = pl.ds(n % 2 * rows, rows)
        to = (g_buf.at[at], m_ref.at[at]) if n < 2 else (g_ref.at[at], e_ref.at[at])
        copies.append(copies_of(quarter, rows, g_hbm, e_hbm, *to, sems.at[n]))
    start(copies[:3])
    q_copy.wait()
    factors = factors_of(q_buf, devices)
    for n, out in enumerate((send, keep)):
        wait(copies[n : n + 1])
        if n == 0:
            start(copies[3:])
        at = slice(n * rows, (n + 1) * rows)
        m = m_ref[at] + g_buf[at].astype(F32)
        m_ref[at] = m
        products(factors[n], m, mh_ref, ml_ref, at, out)
    wait(copies[2:])


def left_rest_kernel(q_ref, e_ref, g_ref, m_ref, mh_ref, ml_ref, send, keep, *, devices):
    rows = send.shape[2]
    factors = factors_of(q_ref, devices)
    for n, out in enumerate((send, keep)):
        at = slice(n * rows, (n + 1) * rows)
        m = e_ref[at] + g_ref[at].astype(F32)
        m_ref[at] = m
        products(factors[n], m, mh_ref, ml_ref, at, out)


def factors_of(q_ref, devices):
    half = q_ref.shape[0] // 2
    out = []
    for _, bit in sides(devices)[::-1]:
        out.append(stack(split(stack([q_ref[pl.ds(pl.multiple_of(at * half, half), half), :] for at in (1 - bit, bit)]), 3)))
    return out


def products(q, m, mh_ref, ml_ref, at, out):
    mh, ml = split(m, 2)
    mh_ref[at] = mh
    ml_ref[at] = ml
    half = out.shape[1]
    p = fold(dot(q, mh, (1, 1)) + dot(q, ml, (1, 1)), 2 * half)
    out[0] = p[:half]
    out[1] = p[half:]


def whole(own, other, bit):
    a, b = own[...], other[...]
    return stack([jnp.where(bit == 0, a, b), jnp.where(bit == 0, b, a)])


def square(p, rank):
    g = fold(dot(p, p, (1, 1)), rank)
    return g[:, :rank] + g[:, rank : 2 * rank] + g[:, 2 * rank :]


def terms_of(pieces):
    return jnp.concatenate([stack(split(x, 3)) for x in pieces], axis=1)


def pair_up(refs, owners, devices):
    return [whole(refs[2 * n], refs[2 * n + 1], sides(devices)[owner][1]) for n, owner in enumerate(owners)]


def right_kernel(*refs, owners, start, first, devices):
    pieces, (mh_ref, ml_ref, *rest) = refs[: 2 * len(owners)], refs[2 * len(owners) :]
    rows = pieces[0].shape[1]
    rank = 2 * pieces[0].shape[0]
    p = terms_of(pair_up(pieces, owners, devices))
    at = slice(start * rows, (start + len(owners)) * rows)
    t = fold(dot(p, mh_ref[at], (1, 0)) + dot(p, ml_ref[at], (1, 0)), rank)
    if first:
        t_ref, gram_ref = rest
        t_ref[...] = t
        gram_ref[...] = square(p, rank)
    else:
        before, t_ref = rest
        t_ref[...] = before[...] + t


def eliminate(a, pivots):
    rank = a.shape[0]
    row = lax.broadcasted_iota(jnp.int32, (rank, 1), 0)
    for k in pivots:
        line = a[k : k + 1, :] / a[k : k + 1, k : k + 1]
        a = a - jnp.where(row > k, a[:, k : k + 1], 0.0) * line
    return a


def factor_kernel(gram_ref, *refs, devices):
    pieces, (state_ref,) = refs[:4], refs[4:]
    rank = gram_ref.shape[0]
    gram = gram_ref[...] + square(terms_of(pair_up(pieces, (1, 0), devices)), rank)
    row = lax.broadcasted_iota(jnp.int32, (rank, 128), 0)
    lane = lax.broadcasted_iota(jnp.int32, (rank, 128), 1)
    eye = (lane == row + rank).astype(F32)
    state_ref[...] = eliminate(jnp.concatenate([gram, eye[:, rank:]], axis=1), range(rank // 2))


def inverse_kernel(state_ref, inv_ref):
    rank = state_ref.shape[0]
    a = eliminate(state_ref[...], range(rank // 2, rank - 1))
    row = lax.broadcasted_iota(jnp.int32, a.shape, 0)
    lane = lax.broadcasted_iota(jnp.int32, a.shape, 1)
    pivots = jnp.sum(jnp.where(row == lane, a, 0.0), axis=1, keepdims=True)
    inv_ref[...] = a[:, rank : 2 * rank] / jnp.sqrt(pivots)


def hat_kernel(inv_ref, *refs, devices):
    hat_ref, rows_ref = refs[8:]
    rows = refs[0].shape[1]
    pieces = pair_up(refs[:8], (1, 0, 1, 0), devices)
    inverse = inv_ref[...]
    left, back = six_left(inverse), six_left(inverse.T)
    for n, quarter in enumerate(order(devices)):
        hat = dot(left, six_right(pieces[n]), (1, 0))
        hat_ref[:, pl.ds(pl.multiple_of(quarter * rows, rows), rows)] = hat
        u, v = split(dot(back, six_right(hat), (1, 0)), 2)
        rows_ref[n * rows : (n + 1) * rows, :] = stack([u, v, u, v]).T


def error_kernel(t0_ref, t1_ref, inv_ref, rows_ref, m_ref, m2_ref, out_hbm, q_hbm, buf, q_buf, sems, q_sem, *, replicas, block, devices):
    t = (t0_ref[...] + t1_ref[...]) / replicas
    u, v = split(t, 2)
    terms = stack([u, u, v, v])
    quarters = order(devices)
    rows = buf.shape[0] // 4
    copies = []
    for n in range(buf.shape[0] // block):
        at = n * block
        quarter, inside = at // rows, at % rows
        source, shift = (m_ref, 0) if quarter < 2 else (m2_ref, 2 * rows)
        buf[at : at + block] = source[at - shift : at - shift + block] - dot(rows_ref[at : at + block], terms, (1, 0))
        to = pl.ds(pl.multiple_of(quarters[quarter] * rows + inside, block), block)
        copy = pltpu.make_async_copy(buf.at[pl.ds(at, block)], out_hbm.at[to], sems.at[n])
        copy.start()
        copies.append(copy)
    q_buf[...] = dot(six_left(inv_ref[...]), six_right(t), (1, 0))
    copies.append(pltpu.make_async_copy(q_buf, q_hbm, q_sem))
    copies[-1].start()
    for copy in copies:
        copy.wait()


def shards(gradient, error_buffer, q_given):
    replicas, tensors = lax.axis_size("dp"), lax.axis_size("tensor")
    devices = replicas * tensors
    depth, columns = gradient.shape[1:]
    rank = q_given.shape[1]
    rows = depth // 4

    def call(kernel, name, flops, **kw):
        made = pl.pallas_call(
            kernel,
            name=name,
            compiler_params=pltpu.CompilerParams(vmem_limit_bytes=LIMIT),
            cost_estimate=pl.CostEstimate(flops=flops, bytes_accessed=0, transcendentals=0),
            **kw,
        )
        spaces = [pltpu.HBM if spec is HBM else pltpu.VMEM for spec in kw["in_specs"]]
        return lambda *args: made(*(pltpu.with_memory_space_constraint(x, space) for x, space in zip(args, spaces, strict=True)))

    piece = pltpu.VMEM((2, rank // 2, rows), F32)
    small = pltpu.VMEM((rank, rank), F32)
    wide = pltpu.VMEM((rank, columns), F32)
    work = 6 * depth * columns * rank

    merged = tuple(pltpu.VMEM((2 * rows, columns), kind) for kind in (F32, BF16, BF16))

    m, mh, ml, e2, g2, send_a, keep_a = call(
        functools.partial(left_kernel, devices=devices),
        "left_products",
        work,
        out_shape=merged + merged[:2] + (piece,) * 2,
        in_specs=[HBM] * 3,
        out_specs=(VMEM,) * 7,
        scratch_shapes=[
            pltpu.VMEM((rank, columns), F32),
            pltpu.VMEM((2 * rows, columns), BF16),
            pltpu.SemaphoreType.DMA(()),
            pltpu.SemaphoreType.DMA((4, 2)),
        ],
    )(q_given.T, gradient[0], error_buffer[0])
    m2, mh2, ml2, send_b, keep_b = call(
        functools.partial(left_rest_kernel, devices=devices),
        "left_products_rest",
        work,
        out_shape=merged + (piece,) * 2,
        in_specs=[VMEM] * 3,
        out_specs=(VMEM,) * 5,
    )(q_given.T, e2, g2)

    def swap(x, bit, bit1=None):
        choice = (bit, bit if bit1 is None else bit1)
        return lax.ppermute(x, AXES, [(i, i ^ choice[i & 1]) for i in range(devices)])

    walk = list(zip(*walks(devices), strict=True))
    sums = [keep + swap(send, 1) for send, keep in ((send_a, keep_a), (send_b, keep_b))]
    arrived = [swap(x[0], *walk[0]) for x in sums]
    own = [x[1] + y for x, y in zip(sums, arrived, strict=True)]
    for bits in walk[1:]:
        arrived = [swap(x, *bits) for x in own]
        own = [x + y for x, y in zip(own, arrived, strict=True)]
    other = [swap(x, *walk[0]) for x in own]
    mine = list(zip(own, other, strict=True))
    theirs = [tuple(swap(x, 1) for x in pair) for pair in mine]

    def right(name, owners, start, pieces, *args):
        first = len(args) == 2
        return call(
            functools.partial(right_kernel, owners=owners, start=start, first=first, devices=devices),
            name,
            work,
            out_shape=(wide, small) if first else wide,
            in_specs=[VMEM] * (len(pieces) + len(args)),
            out_specs=(VMEM, VMEM) if first else VMEM,
        )(*pieces, *args)

    t, gram = right("right_products", (1, 0), 0, theirs[0] + mine[0], mh, ml)
    t = right("right_products_own", (0,), 1, mine[1], mh2, ml2, t)
    t = right("right_products_other", (1,), 0, theirs[1], mh2, ml2, t)

    state = call(
        functools.partial(factor_kernel, devices=devices),
        "factor_first_half",
        work,
        out_shape=pltpu.VMEM((rank, 128), F32),
        in_specs=[VMEM] * 5,
        out_specs=VMEM,
    )(gram, *theirs[1], *mine[1])
    inverse = call(inverse_kernel, "factor_second_half", work, out_shape=small, in_specs=[VMEM], out_specs=VMEM)(state)
    hat, hat_rows = call(
        functools.partial(hat_kernel, devices=devices),
        "left_factor",
        work,
        out_shape=(jax.ShapeDtypeStruct((rank, depth), F32), pltpu.VMEM((depth, 4 * rank), BF16)),
        in_specs=[VMEM] * 9,
        out_specs=(VMEM, VMEM),
    )(inverse, *theirs[0], *mine[0], *theirs[1], *mine[1])

    bits = [bit for bit in walks(devices)[0] if bit >= tensors]
    beside = [state, inverse]
    got = swap(t, bits[0])
    for n, bit in enumerate(bits[1:]):
        t = t + got
        if n < len(beside):
            t, _ = lax.optimization_barrier((t, beside[n]))
        got = swap(t, bit)

    block = rows // 3
    error, q_new = call(
        functools.partial(error_kernel, replicas=replicas, block=block, devices=devices),
        "new_error",
        work,
        out_shape=(pltpu.HBM((depth, columns), F32), pltpu.HBM((rank, columns), F32)),
        in_specs=[VMEM] * 6,
        out_specs=(HBM, HBM),
        scratch_shapes=[
            pltpu.VMEM((depth, columns), F32),
            pltpu.VMEM((rank, columns), F32),
            pltpu.SemaphoreType.DMA((depth // block,)),
            pltpu.SemaphoreType.DMA(()),
        ],
    )(t, got, inverse, hat_rows, m, m2)
    return (error[None], hat.T, q_new.T)


def solution(mesh):
    placed = (P("dp", None, "tensor"), P("dp", None, "tensor"), P("tensor", None))
    return jax.shard_map(
        shards,
        mesh=mesh,
        in_specs=placed,
        out_specs=(P("dp", None, "tensor"), P(), P("tensor", None)),
        check_vma=False,
    )
```

```python
import functools

import jax
import jax.numpy as jnp
from jax import lax
from jax.experimental import pallas as pl
from jax.experimental.pallas import tpu as pltpu
from jax.sharding import PartitionSpec as P

F32, BF16 = jnp.float32, jnp.bfloat16
VMEM = pl.BlockSpec(memory_space=pltpu.VMEM)
HBM = pl.BlockSpec(memory_space=pltpu.HBM)
AXES = ("dp", "tensor")
LIMIT = 12 * 2**20
UNITS = 6


def split(x, terms):
    out = []
    for _ in range(terms):
        t = x.astype(BF16)
        out.append(t)
        x = x - t.astype(F32)
    return out


def stack(terms):
    return jnp.concatenate(terms, axis=0)


def dot(a, b, contract):
    return lax.dot_general(a, b, ((contract[:1], contract[1:]), ((), ())), preferred_element_type=F32)


def fold(x, rank):
    return functools.reduce(jnp.add, [x[i : i + rank] for i in range(0, x.shape[0], rank)])


def six_left(x):
    a, b, c = split(x, 3)
    return jnp.concatenate([a, a, b, a, b, c], axis=1)


def six_right(x):
    u, v, w = split(x, 3)
    return stack([u, v, u, w, v, u])


def walks(devices):
    bits = []
    bit = 2
    while bit < devices:
        bits.append(bit)
        bit *= 2
    walk = bits[::2] + bits[1::2]
    return walk, walk[1:] + walk[:1]


def sides(devices):
    place = lax.axis_index("dp") * lax.axis_size("tensor") + lax.axis_index("tensor")
    core = place & 1
    first, second = ((place >> (walk[0].bit_length() - 1)) & 1 for walk in walks(devices))
    return (1 - core, jnp.where(core == 0, second, first)), (core, jnp.where(core == 0, first, second))


def start(pairs):
    for pair in pairs:
        for copy in pair:
            copy.start()


def wait(pairs):
    for pair in pairs:
        for copy in pair:
            copy.wait()


def left_kernel(q_hbm, g_hbm, e_hbm, m_ref, mh_ref, ml_ref, e_ref, g_ref, send_a, send_b, q_buf, g_buf, q_sem, sems, *, devices):
    theirs, mine = sides(devices)
    half = e_ref.shape[0]
    block = half // 2
    q_copy = pltpu.make_async_copy(q_hbm, q_buf, q_sem)
    q_copy.start()
    copies = []
    for n in range(4):
        source = pl.ds(pl.multiple_of((mine if n > 1 else theirs)[0] * half + n % 2 * block, block), block)
        to = pl.ds(n % 2 * block, block)
        copies.append(
            (
                pltpu.make_async_copy(g_hbm.at[source], (g_ref if n > 1 else g_buf).at[to], sems.at[n, 0]),
                pltpu.make_async_copy(e_hbm.at[source], (e_ref if n > 1 else m_ref).at[to], sems.at[n, 1]),
            )
        )
    start(copies[:3])
    q_copy.wait()
    q = stack(split(q_buf[...], 3))
    for n in range(2):
        wait(copies[n : n + 1])
        if n == 0:
            start(copies[3:])
        at = slice(n * block, (n + 1) * block)
        m = m_ref[at] + g_buf[at].astype(F32)
        m_ref[at] = m
        place(products(q, m, mh_ref, ml_ref, at), n * block, theirs[1], send_a, send_b)
    wait(copies[2:])


def left_rest_kernel(q_ref, e_ref, g_ref, m_ref, mh_ref, ml_ref, keep_a, keep_b, *, devices):
    _, (_, bit) = sides(devices)
    half = e_ref.shape[0]
    block = half // 2
    q = stack(split(q_ref[...], 3))
    for n in range(2):
        at = slice(n * block, (n + 1) * block)
        m = e_ref[at] + g_ref[at].astype(F32)
        m_ref[at] = m
        place(products(q, m, mh_ref, ml_ref, at), n * block, bit, keep_a, keep_b)


def place(p, start, bit, out_a, out_b):
    rows = out_b.shape[1]
    at = 0
    while at < p.shape[1]:
        unit, inside = (start + at) // rows, (start + at) % rows
        width = min(rows - inside, p.shape[1] - at)
        columns = slice(inside, inside + width)
        if unit == 2:
            out_b[:, columns] = p[:, at : at + width]
        else:
            out_a[1 - bit if unit == 0 else bit, :, columns] = p[:, at : at + width]
        at += width


def products(q, m, mh_ref, ml_ref, at):
    mh, ml = split(m, 2)
    mh_ref[at] = mh
    ml_ref[at] = ml
    return fold(dot(q, mh, (1, 1)) + dot(q, ml, (1, 1)), q.shape[0] // 3)


def square(p, rank):
    g = fold(dot(p, p, (1, 1)), rank)
    return g[:, :rank] + g[:, rank : 2 * rank] + g[:, 2 * rank :]


def terms_of(pieces):
    return jnp.concatenate([stack(split(x[...], 3)) for x in pieces], axis=1)


def unit_at(n, rows):
    return pl.ds(n * rows if isinstance(n, int) else pl.multiple_of(n * rows, rows), rows)


def right_early_kernel(a1, b0, a3, b1, mh_ref, ml_ref, mh2_ref, ml2_ref, t_ref, gram_ref, *, devices):
    rank, rows = a1.shape
    (_, their_bit), (_, bit) = sides(devices)
    t = gram = 0.0
    for ref, unit, hs, ls in ((a3, bit, mh2_ref, ml2_ref), (b1, 2, mh2_ref, ml2_ref), (a1, their_bit, mh_ref, ml_ref), (b0, 2, mh_ref, ml_ref)):
        at = unit_at(unit, rows)
        p = terms_of((ref,))
        t = t + dot(p, hs[at], (1, 0)) + dot(p, ls[at], (1, 0))
        gram = gram + square(p, rank)
    t_ref[...] = fold(t, rank)
    gram_ref[...] = gram


def right_kernel(p_ref, mh_ref, ml_ref, before, t_ref, *, side, devices):
    rank, rows = p_ref.shape
    p = terms_of((p_ref,))
    at = unit_at(1 - sides(devices)[side][1], rows)
    t_ref[...] = before[...] + fold(dot(p, mh_ref[at], (1, 0)) + dot(p, ml_ref[at], (1, 0)), rank)


def eliminate(a, pivots):
    rank = a.shape[0]
    row = lax.broadcasted_iota(jnp.int32, (rank, 1), 0)
    for k in pivots:
        line = a[k : k + 1, :] / a[k : k + 1, k : k + 1]
        a = a - jnp.where(row > k, a[:, k : k + 1], 0.0) * line
    return a


def factor_kernel(gram_ref, a0, a2, state_ref):
    rank = gram_ref.shape[0]
    gram = gram_ref[...] + square(terms_of((a0, a2)), rank)
    row = lax.broadcasted_iota(jnp.int32, (rank, 128), 0)
    lane = lax.broadcasted_iota(jnp.int32, (rank, 128), 1)
    eye = (lane == row + rank).astype(F32)
    state_ref[...] = eliminate(jnp.concatenate([gram, eye[:, rank:]], axis=1), range(rank // 2))


def inverse_kernel(state_ref, inv_ref):
    rank = state_ref.shape[0]
    a = eliminate(state_ref[...], range(rank // 2, rank - 1))
    row = lax.broadcasted_iota(jnp.int32, a.shape, 0)
    lane = lax.broadcasted_iota(jnp.int32, a.shape, 1)
    pivots = jnp.sum(jnp.where(row == lane, a, 0.0), axis=1, keepdims=True)
    inv_ref[...] = a[:, rank : 2 * rank] / jnp.sqrt(pivots)


def hat_kernel(inv_ref, *refs, devices):
    pieces, (hat_hbm, rows_ref, hat_buf, sems) = refs[:UNITS], refs[UNITS:]
    rows = pieces[0].shape[1]
    inverse = inv_ref[...]
    left, back = six_left(inverse), six_left(inverse.T)
    copies, units = [], []
    for n, (core, bit) in enumerate(sides(devices)):
        for k, unit in enumerate((1 - bit, bit, 2)):
            i = 3 * n + k
            units.append(3 * n + unit)
            at = pl.ds(i * rows, rows)
            hat_buf[:, at] = dot(left, six_right(pieces[i][...]), (1, 0))
            copies.append(pltpu.make_async_copy(hat_buf.at[:, at], hat_hbm.at[:, unit_at(3 * core + unit, rows)], sems.at[i]))
            copies[-1].start()
    for i in range(UNITS):
        u, v = split(dot(back, six_right(hat_buf[:, i * rows : (i + 1) * rows]), (1, 0)), 2)
        rows_ref[unit_at(units[i], rows), :] = stack([u, v, u, v]).T
    for copy in copies:
        copy.wait()


def error_kernel(t0_ref, t1_ref, inv_ref, rows_ref, m_ref, m2_ref, out_hbm, q_hbm, buf, q_buf, sems, q_sem, *, replicas, block, devices):
    t = (t0_ref[...] + t1_ref[...]) / replicas
    u, v = split(t, 2)
    terms = stack([u, u, v, v])
    half = m_ref.shape[0]
    copies = []
    for source, side, shift in ((m_ref, 0, 0), (m2_ref, 1, half)):
        for at in range(0, half, block):
            here = slice(shift + at, shift + at + block)
            buf[here] = source[at : at + block] - dot(rows_ref[here], terms, (1, 0))
            to = pl.ds(pl.multiple_of(sides(devices)[side][0] * half + at, block), block)
            copies.append(pltpu.make_async_copy(buf.at[pl.ds(shift + at, block)], out_hbm.at[to], sems.at[len(copies)]))
            copies[-1].start()
    q_buf[...] = dot(six_left(inv_ref[...]), six_right(t), (1, 0))
    copies.append(pltpu.make_async_copy(q_buf, q_hbm, q_sem))
    copies[-1].start()
    for copy in copies:
        copy.wait()


def shards(gradient, error_buffer, q_given):
    replicas, tensors = lax.axis_size("dp"), lax.axis_size("tensor")
    devices = replicas * tensors
    depth, columns = gradient.shape[1:]
    rank = q_given.shape[1]
    rows = depth // UNITS

    def call(kernel, name, flops, **kw):
        made = pl.pallas_call(
            kernel,
            name=name,
            compiler_params=pltpu.CompilerParams(vmem_limit_bytes=LIMIT),
            cost_estimate=pl.CostEstimate(flops=flops, bytes_accessed=0, transcendentals=0),
            **kw,
        )
        spaces = [pltpu.HBM if spec is HBM else pltpu.VMEM for spec in kw["in_specs"]]
        return lambda *args: made(*(pltpu.with_memory_space_constraint(x, space) for x, space in zip(args, spaces, strict=True)))

    unit = pltpu.VMEM((rank, rows), F32)
    small = pltpu.VMEM((rank, rank), F32)
    wide = pltpu.VMEM((rank, columns), F32)
    work = 6 * depth * columns * rank

    merged = tuple(pltpu.VMEM((depth // 2, columns), kind) for kind in (F32, BF16, BF16))
    two = pltpu.VMEM((2, rank, rows), F32)
    m, mh, ml, e_own, g_own, send_a, send_b = call(
        functools.partial(left_kernel, devices=devices),
        "left_products",
        work,
        out_shape=merged + merged[:2] + (two, unit),
        in_specs=[HBM] * 3,
        out_specs=(VMEM,) * 7,
        scratch_shapes=[
            pltpu.VMEM((rank, columns), F32),
            pltpu.VMEM((depth // 2, columns), BF16),
            pltpu.SemaphoreType.DMA(()),
            pltpu.SemaphoreType.DMA((4, 2)),
        ],
    )(q_given.T, gradient[0], error_buffer[0])
    m2, mh2, ml2, keep_a, keep_b = call(
        functools.partial(left_rest_kernel, devices=devices),
        "left_products_rest",
        work,
        out_shape=merged + (two, unit),
        in_specs=[VMEM] * 3,
        out_specs=(VMEM,) * 5,
    )(q_given.T, e_own, g_own)

    def swap(x, bit, bit1=None):
        choice = (bit, bit if bit1 is None else bit1)
        return lax.ppermute(x, AXES, [(i, i ^ choice[i & 1]) for i in range(devices)])

    walk = list(zip(*walks(devices), strict=True))
    both = keep_a + swap(send_a, 1)
    b1 = keep_b + swap(send_b, 1)
    sent, a3 = both[0], both[1]
    for n, bits in enumerate(walk):
        arrived = swap(sent if n == 0 else a3, *bits), swap(b1, *bits)
        a3, b1 = a3 + arrived[0], b1 + arrived[1]
    a2 = swap(a3, *walk[0])
    a1, b0, a0 = swap(a3, 1), swap(b1, 1), swap(a2, 1)

    t, gram = call(
        functools.partial(right_early_kernel, devices=devices),
        "right_products",
        work,
        out_shape=(wide, small),
        in_specs=[VMEM] * 8,
        out_specs=(VMEM, VMEM),
    )(a1, b0, a3, b1, mh, ml, mh2, ml2)
    for side, name, x, hs, ls in ((1, "own", a2, mh2, ml2), (0, "other", a0, mh, ml)):
        t = call(
            functools.partial(right_kernel, side=side, devices=devices),
            "right_products_" + name,
            work,
            out_shape=wide,
            in_specs=[VMEM] * 4,
            out_specs=VMEM,
        )(x, hs, ls, t)

    state = call(
        factor_kernel,
        "factor_first_half",
        work,
        out_shape=pltpu.VMEM((rank, 128), F32),
        in_specs=[VMEM] * 3,
        out_specs=VMEM,
    )(gram, a0, a2)
    inverse = call(inverse_kernel, "factor_second_half", work, out_shape=small, in_specs=[VMEM], out_specs=VMEM)(state)
    hat, hat_rows = call(
        functools.partial(hat_kernel, devices=devices),
        "left_factor",
        work,
        out_shape=(pltpu.HBM((rank, depth), F32), pltpu.VMEM((depth, 4 * rank), BF16)),
        in_specs=[VMEM] * (1 + UNITS),
        out_specs=(HBM, VMEM),
        scratch_shapes=[pltpu.VMEM((rank, depth), F32), pltpu.SemaphoreType.DMA((UNITS,))],
    )(inverse, a0, a1, b0, a2, a3, b1)

    bits = sorted(bit for bit in walks(devices)[0] if bit >= tensors)
    beside = [state, inverse]
    got = swap(t, bits[0])
    for n, bit in enumerate(bits[1:]):
        t = t + got
        if n < len(beside):
            t, _ = lax.optimization_barrier((t, beside[n]))
        got = swap(t, bit)

    block = rows // 2
    error, q_new = call(
        functools.partial(error_kernel, replicas=replicas, block=block, devices=devices),
        "new_error",
        work,
        out_shape=(pltpu.HBM((depth, columns), F32), pltpu.HBM((rank, columns), F32)),
        in_specs=[VMEM] * 6,
        out_specs=(HBM, HBM),
        scratch_shapes=[
            pltpu.VMEM((depth, columns), F32),
            pltpu.VMEM((rank, columns), F32),
            pltpu.SemaphoreType.DMA((depth // block,)),
            pltpu.SemaphoreType.DMA(()),
        ],
    )(t, got, inverse, hat_rows, m, m2)
    return (error[None], hat.T, q_new.T)


def solution(mesh):
    placed = (P("dp", None, "tensor"), P("dp", None, "tensor"), P("tensor", None))
    return jax.shard_map(
        shards,
        mesh=mesh,
        in_specs=placed,
        out_specs=(P("dp", None, "tensor"), P(), P("tensor", None)),
        check_vma=False,
    )
```

```python
import functools

import jax
import jax.numpy as jnp
from jax import lax
from jax.experimental import pallas as pl
from jax.experimental.pallas import tpu as pltpu
from jax.sharding import PartitionSpec as P

F32, BF16 = jnp.float32, jnp.bfloat16
VMEM = pl.BlockSpec(memory_space=pltpu.VMEM)
HBM = pl.BlockSpec(memory_space=pltpu.HBM)
AXES = ("dp", "tensor")
LIMIT = 12 * 2**20
UNITS = 6


def split(x, terms):
    out = []
    for _ in range(terms):
        t = x.astype(BF16)
        out.append(t)
        x = x - t.astype(F32)
    return out


def stack(terms):
    return jnp.concatenate(terms, axis=0)


def dot(a, b, contract):
    return lax.dot_general(a, b, ((contract[:1], contract[1:]), ((), ())), preferred_element_type=F32)


def fold(x, rank):
    return functools.reduce(jnp.add, [x[i : i + rank] for i in range(0, x.shape[0], rank)])


def six_left(x):
    a, b, c = split(x, 3)
    return jnp.concatenate([a, a, b, a, b, c], axis=1)


def six_right(x):
    u, v, w = split(x, 3)
    return stack([u, v, u, w, v, u])


def walks(devices):
    bits = []
    bit = 2
    while bit < devices:
        bits.append(bit)
        bit *= 2
    walk = bits[::2] + bits[1::2]
    return walk, walk[1:] + walk[:1]


def role(place):
    return place.bit_count() & 1


def sides(devices):
    place = lax.axis_index("dp") * lax.axis_size("tensor") + lax.axis_index("tensor")
    half = 0
    for n in range(devices.bit_length() - 1):
        half = half ^ ((place >> n) & 1)
    first, second = ((place >> (walk[0].bit_length() - 1)) & 1 for walk in walks(devices))
    return (1 - half, jnp.where(half == 0, second, first)), (half, jnp.where(half == 0, first, second))


def start(pairs):
    for pair in pairs:
        for copy in pair:
            copy.start()


def wait(pairs):
    for pair in pairs:
        for copy in pair:
            copy.wait()


def left_kernel(q_hbm, g_hbm, e_hbm, m_ref, mh_ref, ml_ref, e_ref, g_ref, send_a, send_b, q_buf, g_buf, q_sem, sems, *, devices):
    theirs, mine = sides(devices)
    half = e_ref.shape[0]
    block = half // 2
    q_copy = pltpu.make_async_copy(q_hbm, q_buf, q_sem)
    q_copy.start()
    copies = []
    for n in range(4):
        source = pl.ds(pl.multiple_of((mine if n > 1 else theirs)[0] * half + n % 2 * block, block), block)
        to = pl.ds(n % 2 * block, block)
        copies.append(
            (
                pltpu.make_async_copy(g_hbm.at[source], (g_ref if n > 1 else g_buf).at[to], sems.at[n, 0]),
                pltpu.make_async_copy(e_hbm.at[source], (e_ref if n > 1 else m_ref).at[to], sems.at[n, 1]),
            )
        )
    start(copies[:3])
    q_copy.wait()
    q = stack(split(q_buf[...], 3))
    for n in range(2):
        wait(copies[n : n + 1])
        if n == 0:
            start(copies[3:])
        at = slice(n * block, (n + 1) * block)
        m = m_ref[at] + g_buf[at].astype(F32)
        m_ref[at] = m
        place(products(q, m, mh_ref, ml_ref, at), n * block, theirs[1], send_a, send_b)
    wait(copies[2:])


def left_rest_kernel(q_ref, e_ref, g_ref, m_ref, mh_ref, ml_ref, keep_a, keep_b, *, devices):
    _, (_, bit) = sides(devices)
    half = e_ref.shape[0]
    block = half // 2
    q = stack(split(q_ref[...], 3))
    for n in range(2):
        at = slice(n * block, (n + 1) * block)
        m = e_ref[at] + g_ref[at].astype(F32)
        m_ref[at] = m
        place(products(q, m, mh_ref, ml_ref, at), n * block, bit, keep_a, keep_b)


def place(p, start, bit, out_a, out_b):
    rows = out_b.shape[1]
    at = 0
    while at < p.shape[1]:
        unit, inside = (start + at) // rows, (start + at) % rows
        width = min(rows - inside, p.shape[1] - at)
        columns = slice(inside, inside + width)
        if unit == 2:
            out_b[:, columns] = p[:, at : at + width]
        else:
            out_a[1 - bit if unit == 0 else bit, :, columns] = p[:, at : at + width]
        at += width


def products(q, m, mh_ref, ml_ref, at):
    mh, ml = split(m, 2)
    mh_ref[at] = mh
    ml_ref[at] = ml
    return fold(dot(q, mh, (1, 1)) + dot(q, ml, (1, 1)), q.shape[0] // 3)


def square(p, rank):
    g = fold(dot(p, p, (1, 1)), rank)
    return g[:, :rank] + g[:, rank : 2 * rank] + g[:, 2 * rank :]


def terms_of(pieces):
    return jnp.concatenate([stack(split(x[...], 3)) for x in pieces], axis=1)


def unit_at(n, rows):
    return pl.ds(n * rows if isinstance(n, int) else pl.multiple_of(n * rows, rows), rows)


def right_early_kernel(a1, b0, a3, b1, mh_ref, ml_ref, mh2_ref, ml2_ref, t_ref, gram_ref, *, devices):
    rank, rows = a1.shape
    (_, their_bit), (_, bit) = sides(devices)
    t = gram = 0.0
    for ref, unit, hs, ls in ((a3, bit, mh2_ref, ml2_ref), (b1, 2, mh2_ref, ml2_ref), (a1, their_bit, mh_ref, ml_ref), (b0, 2, mh_ref, ml_ref)):
        at = unit_at(unit, rows)
        p = terms_of((ref,))
        t = t + dot(p, hs[at], (1, 0)) + dot(p, ls[at], (1, 0))
        gram = gram + square(p, rank)
    t_ref[...] = fold(t, rank)
    gram_ref[...] = gram


def right_kernel(p_ref, mh_ref, ml_ref, before, t_ref, *, side, devices):
    rank, rows = p_ref.shape
    p = terms_of((p_ref,))
    at = unit_at(1 - sides(devices)[side][1], rows)
    t_ref[...] = before[...] + fold(dot(p, mh_ref[at], (1, 0)) + dot(p, ml_ref[at], (1, 0)), rank)


def eliminate(a, pivots):
    rank = a.shape[0]
    row = lax.broadcasted_iota(jnp.int32, (rank, 1), 0)
    for k in pivots:
        line = a[k : k + 1, :] / a[k : k + 1, k : k + 1]
        a = a - jnp.where(row > k, a[:, k : k + 1], 0.0) * line
    return a


def factor_kernel(gram_ref, a0, a2, state_ref):
    rank = gram_ref.shape[0]
    gram = gram_ref[...] + square(terms_of((a0, a2)), rank)
    row = lax.broadcasted_iota(jnp.int32, (rank, 128), 0)
    lane = lax.broadcasted_iota(jnp.int32, (rank, 128), 1)
    eye = (lane == row + rank).astype(F32)
    state_ref[...] = eliminate(jnp.concatenate([gram, eye[:, rank:]], axis=1), range(rank // 2))


def inverse_kernel(state_ref, inv_ref):
    rank = state_ref.shape[0]
    a = eliminate(state_ref[...], range(rank // 2, rank - 1))
    row = lax.broadcasted_iota(jnp.int32, a.shape, 0)
    lane = lax.broadcasted_iota(jnp.int32, a.shape, 1)
    pivots = jnp.sum(jnp.where(row == lane, a, 0.0), axis=1, keepdims=True)
    inv_ref[...] = a[:, rank : 2 * rank] / jnp.sqrt(pivots)


def hat_kernel(inv_ref, *refs, devices):
    pieces, (hat_hbm, rows_ref, hat_buf, sems) = refs[:UNITS], refs[UNITS:]
    rows = pieces[0].shape[1]
    inverse = inv_ref[...]
    left, back = six_left(inverse), six_left(inverse.T)
    copies, units = [], []
    for n, (core, bit) in enumerate(sides(devices)):
        for k, unit in enumerate((1 - bit, bit, 2)):
            i = 3 * n + k
            units.append(3 * n + unit)
            at = pl.ds(i * rows, rows)
            hat_buf[:, at] = dot(left, six_right(pieces[i][...]), (1, 0))
            copies.append(pltpu.make_async_copy(hat_buf.at[:, at], hat_hbm.at[:, unit_at(3 * core + unit, rows)], sems.at[i]))
            copies[-1].start()
    for i in range(UNITS):
        u, v = split(dot(back, six_right(hat_buf[:, i * rows : (i + 1) * rows]), (1, 0)), 2)
        rows_ref[unit_at(units[i], rows), :] = stack([u, v, u, v]).T
    for copy in copies:
        copy.wait()


def error_kernel(t0_ref, t1_ref, inv_ref, rows_ref, m_ref, m2_ref, out_hbm, q_hbm, buf, q_buf, sems, q_sem, *, replicas, block, devices):
    t = (t0_ref[...] + t1_ref[...]) / replicas
    u, v = split(t, 2)
    terms = stack([u, u, v, v])
    half = m_ref.shape[0]
    copies = []
    for source, side, shift in ((m_ref, 0, 0), (m2_ref, 1, half)):
        for at in range(0, half, block):
            here = slice(shift + at, shift + at + block)
            buf[here] = source[at : at + block] - dot(rows_ref[here], terms, (1, 0))
            to = pl.ds(pl.multiple_of(sides(devices)[side][0] * half + at, block), block)
            copies.append(pltpu.make_async_copy(buf.at[pl.ds(shift + at, block)], out_hbm.at[to], sems.at[len(copies)]))
            copies[-1].start()
    q_buf[...] = dot(six_left(inv_ref[...]), six_right(t), (1, 0))
    copies.append(pltpu.make_async_copy(q_buf, q_hbm, q_sem))
    copies[-1].start()
    for copy in copies:
        copy.wait()


def shards(gradient, error_buffer, q_given):
    replicas, tensors = lax.axis_size("dp"), lax.axis_size("tensor")
    devices = replicas * tensors
    depth, columns = gradient.shape[1:]
    rank = q_given.shape[1]
    rows = depth // UNITS

    def call(kernel, name, flops, **kw):
        made = pl.pallas_call(
            kernel,
            name=name,
            compiler_params=pltpu.CompilerParams(vmem_limit_bytes=LIMIT),
            cost_estimate=pl.CostEstimate(flops=flops, bytes_accessed=0, transcendentals=0),
            **kw,
        )
        spaces = [pltpu.HBM if spec is HBM else pltpu.VMEM for spec in kw["in_specs"]]
        return lambda *args: made(*(pltpu.with_memory_space_constraint(x, space) for x, space in zip(args, spaces, strict=True)))

    unit = pltpu.VMEM((rank, rows), F32)
    small = pltpu.VMEM((rank, rank), F32)
    wide = pltpu.VMEM((rank, columns), F32)
    work = 6 * depth * columns * rank

    merged = tuple(pltpu.VMEM((depth // 2, columns), kind) for kind in (F32, BF16, BF16))
    two = pltpu.VMEM((2, rank, rows), F32)
    m, mh, ml, e_own, g_own, send_a, send_b = call(
        functools.partial(left_kernel, devices=devices),
        "left_products",
        work,
        out_shape=merged + merged[:2] + (two, unit),
        in_specs=[HBM] * 3,
        out_specs=(VMEM,) * 7,
        scratch_shapes=[
            pltpu.VMEM((rank, columns), F32),
            pltpu.VMEM((depth // 2, columns), BF16),
            pltpu.SemaphoreType.DMA(()),
            pltpu.SemaphoreType.DMA((4, 2)),
        ],
    )(q_given.T, gradient[0], error_buffer[0])
    m2, mh2, ml2, keep_a, keep_b = call(
        functools.partial(left_rest_kernel, devices=devices),
        "left_products_rest",
        work,
        out_shape=merged + (two, unit),
        in_specs=[VMEM] * 3,
        out_specs=(VMEM,) * 5,
    )(q_given.T, e_own, g_own)

    def swap(x, bit):
        return lax.ppermute(x, AXES, [(i, i ^ bit) for i in range(devices)])

    def cross(x, *bits):
        return lax.ppermute(x, AXES, [(i, i ^ 1 ^ bits[role(i)]) for i in range(devices)])

    walk = list(zip(*walks(devices), strict=True))
    both = keep_a + swap(send_a, 1)
    b1 = keep_b + swap(send_b, 1)
    sent, a3 = both[0], both[1]
    for n, bits in enumerate(walk):
        arrived = cross(sent if n == 0 else a3, *bits), cross(b1, *bits)
        a3, b1 = a3 + arrived[0], b1 + arrived[1]
    a2 = cross(a3, *walk[0])
    a1, b0, a0 = swap(a3, 1), swap(b1, 1), swap(a2, 1)

    t, gram = call(
        functools.partial(right_early_kernel, devices=devices),
        "right_products",
        work,
        out_shape=(wide, small),
        in_specs=[VMEM] * 8,
        out_specs=(VMEM, VMEM),
    )(a1, b0, a3, b1, mh, ml, mh2, ml2)
    for side, name, x, hs, ls in ((1, "own", a2, mh2, ml2), (0, "other", a0, mh, ml)):
        t = call(
            functools.partial(right_kernel, side=side, devices=devices),
            "right_products_" + name,
            work,
            out_shape=wide,
            in_specs=[VMEM] * 4,
            out_specs=VMEM,
        )(x, hs, ls, t)

    state = call(
        factor_kernel,
        "factor_first_half",
        work,
        out_shape=pltpu.VMEM((rank, 128), F32),
        in_specs=[VMEM] * 3,
        out_specs=VMEM,
    )(gram, a0, a2)
    inverse = call(inverse_kernel, "factor_second_half", work, out_shape=small, in_specs=[VMEM], out_specs=VMEM)(state)
    hat, hat_rows = call(
        functools.partial(hat_kernel, devices=devices),
        "left_factor",
        work,
        out_shape=(pltpu.HBM((rank, depth), F32), pltpu.VMEM((depth, 4 * rank), BF16)),
        in_specs=[VMEM] * (1 + UNITS),
        out_specs=(HBM, VMEM),
        scratch_shapes=[pltpu.VMEM((rank, depth), F32), pltpu.SemaphoreType.DMA((UNITS,))],
    )(inverse, a0, a1, b0, a2, a3, b1)

    bits = sorted(bit for bit in walks(devices)[0] if bit >= tensors)
    beside = [state, inverse]
    got = swap(t, bits[0])
    for n, bit in enumerate(bits[1:]):
        t = t + got
        if n < len(beside):
            t, _ = lax.optimization_barrier((t, beside[n]))
        got = swap(t, bit)

    block = rows // 2
    error, q_new = call(
        functools.partial(error_kernel, replicas=replicas, block=block, devices=devices),
        "new_error",
        work,
        out_shape=(pltpu.HBM((depth, columns), F32), pltpu.HBM((rank, columns), F32)),
        in_specs=[VMEM] * 6,
        out_specs=(HBM, HBM),
        scratch_shapes=[
            pltpu.VMEM((depth, columns), F32),
            pltpu.VMEM((rank, columns), F32),
            pltpu.SemaphoreType.DMA((depth // block,)),
            pltpu.SemaphoreType.DMA(()),
        ],
    )(t, got, inverse, hat_rows, m, m2)
    return (error[None], hat.T, q_new.T)


def solution(mesh):
    placed = (P("dp", None, "tensor"), P("dp", None, "tensor"), P("tensor", None))
    return jax.shard_map(
        shards,
        mesh=mesh,
        in_specs=placed,
        out_specs=(P("dp", None, "tensor"), P(), P("tensor", None)),
        check_vma=False,
    )
```

```python
import functools

import jax
import jax.numpy as jnp
from jax import lax
from jax.experimental import pallas as pl
from jax.experimental.pallas import tpu as pltpu
from jax.sharding import PartitionSpec as P

F32, BF16 = jnp.float32, jnp.bfloat16
VMEM = pl.BlockSpec(memory_space=pltpu.VMEM)
HBM = pl.BlockSpec(memory_space=pltpu.HBM)
AXES = ("dp", "tensor")
LIMIT = 12 * 2**20
UNITS = 6


def split(x, terms):
    out = []
    for _ in range(terms):
        t = x.astype(BF16)
        out.append(t)
        x = x - t.astype(F32)
    return out


def stack(terms):
    return jnp.concatenate(terms, axis=0)


def dot(a, b, contract):
    return lax.dot_general(a, b, ((contract[:1], contract[1:]), ((), ())), preferred_element_type=F32)


def fold(x, rank):
    return functools.reduce(jnp.add, [x[i : i + rank] for i in range(0, x.shape[0], rank)])


def six_left(x):
    a, b, c = split(x, 3)
    return jnp.concatenate([a, a, b, a, b, c], axis=1)


def six_right(x):
    u, v, w = split(x, 3)
    return stack([u, v, u, w, v, u])


def walks(devices):
    bits = []
    bit = 2
    while bit < devices:
        bits.append(bit)
        bit *= 2
    walk = bits[::2] + bits[1::2]
    return walk, walk[1:] + walk[:1]


def role(place):
    return place.bit_count() & 1


def sides(devices):
    place = lax.axis_index("dp") * lax.axis_size("tensor") + lax.axis_index("tensor")
    half = 0
    for n in range(devices.bit_length() - 1):
        half = half ^ ((place >> n) & 1)
    first, second = ((place >> (walk[0].bit_length() - 1)) & 1 for walk in walks(devices))
    return (1 - half, jnp.where(half == 0, second, first)), (half, jnp.where(half == 0, first, second))


def start(pairs):
    for pair in pairs:
        for copy in pair:
            copy.start()


def wait(pairs):
    for pair in pairs:
        for copy in pair:
            copy.wait()


def left_kernel(q_hbm, g_hbm, e_hbm, m_ref, mh_ref, ml_ref, e_ref, g_ref, send_a, send_b, q_buf, g_buf, q_sem, sems, *, devices):
    theirs, mine = sides(devices)
    half = e_ref.shape[0]
    block = half // 2
    q_copy = pltpu.make_async_copy(q_hbm, q_buf, q_sem)
    q_copy.start()
    copies = []
    for n in range(4):
        source = pl.ds(pl.multiple_of((mine if n > 1 else theirs)[0] * half + n % 2 * block, block), block)
        to = pl.ds(n % 2 * block, block)
        copies.append(
            (
                pltpu.make_async_copy(g_hbm.at[source], (g_ref if n > 1 else g_buf).at[to], sems.at[n, 0]),
                pltpu.make_async_copy(e_hbm.at[source], (e_ref if n > 1 else m_ref).at[to], sems.at[n, 1]),
            )
        )
    start(copies[:3])
    q_copy.wait()
    q = stack(split(q_buf[...], 3))
    for n in range(2):
        wait(copies[n : n + 1])
        if n == 0:
            start(copies[3:])
        at = slice(n * block, (n + 1) * block)
        m = m_ref[at] + g_buf[at].astype(F32)
        m_ref[at] = m
        place(products(q, m, mh_ref, ml_ref, at), n * block, theirs[1], send_a, send_b)
    wait(copies[2:])


def left_rest_kernel(q_ref, e_ref, g_ref, m_ref, mh_ref, ml_ref, keep_a, keep_b, *, devices):
    _, (_, bit) = sides(devices)
    half = e_ref.shape[0]
    block = half // 2
    q = stack(split(q_ref[...], 3))
    for n in range(2):
        at = slice(n * block, (n + 1) * block)
        m = e_ref[at] + g_ref[at].astype(F32)
        m_ref[at] = m
        place(products(q, m, mh_ref, ml_ref, at), n * block, bit, keep_a, keep_b)


def place(p, start, bit, out_a, out_b):
    rows = out_b.shape[1]
    at = 0
    while at < p.shape[1]:
        unit, inside = (start + at) // rows, (start + at) % rows
        width = min(rows - inside, p.shape[1] - at)
        columns = slice(inside, inside + width)
        if unit == 2:
            out_b[:, columns] = p[:, at : at + width]
        else:
            out_a[1 - bit if unit == 0 else bit, :, columns] = p[:, at : at + width]
        at += width


def products(q, m, mh_ref, ml_ref, at):
    mh, ml = split(m, 2)
    mh_ref[at] = mh
    ml_ref[at] = ml
    return fold(dot(q, mh, (1, 1)) + dot(q, ml, (1, 1)), q.shape[0] // 3)


def square(p, rank):
    g = fold(dot(p, p, (1, 1)), rank)
    return g[:, :rank] + g[:, rank : 2 * rank] + g[:, 2 * rank :]


def terms_of(pieces):
    return jnp.concatenate([stack(split(x[...], 3)) for x in pieces], axis=1)


def unit_at(n, rows):
    return pl.ds(n * rows if isinstance(n, int) else pl.multiple_of(n * rows, rows), rows)


def right_early_kernel(a1, b0, a3, b1, mh_ref, ml_ref, mh2_ref, ml2_ref, t_ref, gram_ref, *, devices):
    rank, rows = a1.shape
    (_, their_bit), (_, bit) = sides(devices)
    t = gram = 0.0
    for ref, unit, hs, ls in ((a3, bit, mh2_ref, ml2_ref), (b1, 2, mh2_ref, ml2_ref), (a1, their_bit, mh_ref, ml_ref), (b0, 2, mh_ref, ml_ref)):
        at = unit_at(unit, rows)
        p = terms_of((ref,))
        t = t + dot(p, hs[at], (1, 0)) + dot(p, ls[at], (1, 0))
        gram = gram + square(p, rank)
    t_ref[...] = fold(t, rank)
    gram_ref[...] = gram


def right_kernel(p_ref, mh_ref, ml_ref, before, t_ref, *, side, devices):
    rank, rows = p_ref.shape
    p = terms_of((p_ref,))
    at = unit_at(1 - sides(devices)[side][1], rows)
    t_ref[...] = before[...] + fold(dot(p, mh_ref[at], (1, 0)) + dot(p, ml_ref[at], (1, 0)), rank)


def eliminate(a, pivots):
    rank = a.shape[0]
    row = lax.broadcasted_iota(jnp.int32, (rank, 1), 0)
    for k in pivots:
        line = a[k : k + 1, :] / a[k : k + 1, k : k + 1]
        a = a - jnp.where(row > k, a[:, k : k + 1], 0.0) * line
    return a


def factor_kernel(gram_ref, a0, a2, state_ref):
    rank = gram_ref.shape[0]
    gram = gram_ref[...] + square(terms_of((a0, a2)), rank)
    row = lax.broadcasted_iota(jnp.int32, (rank, 128), 0)
    lane = lax.broadcasted_iota(jnp.int32, (rank, 128), 1)
    eye = (lane == row + rank).astype(F32)
    state_ref[...] = eliminate(jnp.concatenate([gram, eye[:, rank:]], axis=1), range(rank // 2))


def inverse_kernel(state_ref, inv_ref):
    rank = state_ref.shape[0]
    a = eliminate(state_ref[...], range(rank // 2, rank - 1))
    row = lax.broadcasted_iota(jnp.int32, a.shape, 0)
    lane = lax.broadcasted_iota(jnp.int32, a.shape, 1)
    pivots = jnp.sum(jnp.where(row == lane, a, 0.0), axis=1, keepdims=True)
    inv_ref[...] = a[:, rank : 2 * rank] / jnp.sqrt(pivots)


def hat_kernel(inv_ref, *refs, devices):
    pieces, (hat_hbm, rows_ref, hat_buf, sems) = refs[:UNITS], refs[UNITS:]
    rows = pieces[0].shape[1]
    inverse = inv_ref[...]
    left, back = six_left(inverse), six_left(inverse.T)
    copies, units = [], []
    for n, (core, bit) in enumerate(sides(devices)):
        for k, unit in enumerate((1 - bit, bit, 2)):
            i = 3 * n + k
            units.append(3 * n + unit)
            at = pl.ds(i * rows, rows)
            hat_buf[:, at] = dot(left, six_right(pieces[i][...]), (1, 0))
            copies.append(pltpu.make_async_copy(hat_buf.at[:, at], hat_hbm.at[:, unit_at(3 * core + unit, rows)], sems.at[i]))
            copies[-1].start()
    for i in range(UNITS):
        u, v = split(dot(back, six_right(hat_buf[:, i * rows : (i + 1) * rows]), (1, 0)), 2)
        rows_ref[unit_at(units[i], rows), :] = stack([u, v, u, v]).T
    for copy in copies:
        copy.wait()


def error_kernel(t0_ref, t1_ref, inv_ref, rows_ref, m_ref, m2_ref, out_hbm, q_hbm, buf, q_buf, sems, q_sem, *, replicas, block, devices):
    t = (t0_ref[...] + t1_ref[...]) / replicas
    u, v = split(t, 2)
    terms = stack([u, u, v, v])
    half = m_ref.shape[0]
    copies = []
    for source, side, shift in ((m_ref, 0, 0), (m2_ref, 1, half)):
        for at in range(0, half, block):
            here = slice(shift + at, shift + at + block)
            buf[here] = source[at : at + block] - dot(rows_ref[here], terms, (1, 0))
            to = pl.ds(pl.multiple_of(sides(devices)[side][0] * half + at, block), block)
            copies.append(pltpu.make_async_copy(buf.at[pl.ds(shift + at, block)], out_hbm.at[to], sems.at[len(copies)]))
            copies[-1].start()
    q_buf[...] = dot(six_left(inv_ref[...]), six_right(t), (1, 0))
    copies.append(pltpu.make_async_copy(q_buf, q_hbm, q_sem))
    copies[-1].start()
    for copy in copies:
        copy.wait()


def shards(gradient, error_buffer, q_given):
    replicas, tensors = lax.axis_size("dp"), lax.axis_size("tensor")
    devices = replicas * tensors
    depth, columns = gradient.shape[1:]
    rank = q_given.shape[1]
    rows = depth // UNITS

    def call(kernel, name, flops, **kw):
        made = pl.pallas_call(
            kernel,
            name=name,
            compiler_params=pltpu.CompilerParams(vmem_limit_bytes=LIMIT),
            cost_estimate=pl.CostEstimate(flops=flops, bytes_accessed=0, transcendentals=0),
            **kw,
        )
        spaces = [pltpu.HBM if spec is HBM else pltpu.VMEM for spec in kw["in_specs"]]
        return lambda *args: made(*(pltpu.with_memory_space_constraint(x, space) for x, space in zip(args, spaces, strict=True)))

    unit = pltpu.VMEM((rank, rows), F32)
    small = pltpu.VMEM((rank, rank), F32)
    wide = pltpu.VMEM((rank, columns), F32)
    work = 6 * depth * columns * rank

    merged = tuple(pltpu.VMEM((depth // 2, columns), kind) for kind in (F32, BF16, BF16))
    two = pltpu.VMEM((2, rank, rows), F32)
    m, mh, ml, e_own, g_own, send_a, send_b = call(
        functools.partial(left_kernel, devices=devices),
        "left_products",
        work,
        out_shape=merged + merged[:2] + (two, unit),
        in_specs=[HBM] * 3,
        out_specs=(VMEM,) * 7,
        scratch_shapes=[
            pltpu.VMEM((rank, columns), F32),
            pltpu.VMEM((depth // 2, columns), BF16),
            pltpu.SemaphoreType.DMA(()),
            pltpu.SemaphoreType.DMA((4, 2)),
        ],
    )(q_given.T, gradient[0], error_buffer[0])
    m2, mh2, ml2, keep_a, keep_b = call(
        functools.partial(left_rest_kernel, devices=devices),
        "left_products_rest",
        work,
        out_shape=merged + (two, unit),
        in_specs=[VMEM] * 3,
        out_specs=(VMEM,) * 5,
    )(q_given.T, e_own, g_own)

    def swap(x, bit):
        return lax.ppermute(x, AXES, [(i, i ^ bit) for i in range(devices)])

    def cross(x, *bits):
        return lax.ppermute(x, AXES, [(i, i ^ 1 ^ bits[role(i)]) for i in range(devices)])

    walk = list(zip(*walks(devices), strict=True))
    both = keep_a + swap(send_a, 1)
    b1 = keep_b + swap(send_b, 1)
    sent, a3 = both[0], both[1]
    for n, bits in enumerate(walk):
        arrived = cross(sent if n == 0 else a3, *bits), cross(b1, *bits)
        a3, b1 = a3 + arrived[0], b1 + arrived[1]
    a2 = cross(a3, *walk[0])
    a1, b0, a0 = swap(a3, 1), swap(b1, 1), swap(a2, 1)

    t, gram = call(
        functools.partial(right_early_kernel, devices=devices),
        "right_products",
        work,
        out_shape=(wide, small),
        in_specs=[VMEM] * 8,
        out_specs=(VMEM, VMEM),
    )(a1, b0, a3, b1, mh, ml, mh2, ml2)
    for side, name, x, hs, ls in ((1, "own", a2, mh2, ml2), (0, "other", a0, mh, ml)):
        t = call(
            functools.partial(right_kernel, side=side, devices=devices),
            "right_products_" + name,
            work,
            out_shape=wide,
            in_specs=[VMEM] * 4,
            out_specs=VMEM,
        )(x, hs, ls, t)

    state = call(
        factor_kernel,
        "factor_first_half",
        work,
        out_shape=pltpu.VMEM((rank, 128), F32),
        in_specs=[VMEM] * 3,
        out_specs=VMEM,
    )(gram, a0, a2)
    inverse = call(inverse_kernel, "factor_second_half", work, out_shape=small, in_specs=[VMEM], out_specs=VMEM)(state)
    hat, hat_rows = call(
        functools.partial(hat_kernel, devices=devices),
        "left_factor",
        work,
        out_shape=(pltpu.HBM((rank, depth), F32), pltpu.VMEM((depth, 4 * rank), BF16)),
        in_specs=[VMEM] * (1 + UNITS),
        out_specs=(HBM, VMEM),
        scratch_shapes=[pltpu.VMEM((rank, depth), F32), pltpu.SemaphoreType.DMA((UNITS,))],
    )(inverse, a0, a1, b0, a2, a3, b1)

    bits = sorted(bit for bit in walks(devices)[0] if bit >= tensors)
    turns = len(bits) // 2 * 2
    beside = [state, inverse]
    parts = t, None
    for n, bit in enumerate(bits):
        if n:
            t = parts[0] + parts[1]
            if n <= len(beside):
                t, _ = lax.optimization_barrier((t, beside[n - 1]))
        parts = (swap(t, 1), swap(t, 1 ^ bit)) if n < turns else (t, swap(t, bit))

    block = rows // 2
    error, q_new = call(
        functools.partial(error_kernel, replicas=replicas, block=block, devices=devices),
        "new_error",
        work,
        out_shape=(pltpu.HBM((depth, columns), F32), pltpu.HBM((rank, columns), F32)),
        in_specs=[VMEM] * 6,
        out_specs=(HBM, HBM),
        scratch_shapes=[
            pltpu.VMEM((depth, columns), F32),
            pltpu.VMEM((rank, columns), F32),
            pltpu.SemaphoreType.DMA((depth // block,)),
            pltpu.SemaphoreType.DMA(()),
        ],
    )(*parts, inverse, hat_rows, m, m2)
    return (error[None], hat.T, q_new.T)


def solution(mesh):
    placed = (P("dp", None, "tensor"), P("dp", None, "tensor"), P("tensor", None))
    return jax.shard_map(
        shards,
        mesh=mesh,
        in_specs=placed,
        out_specs=(P("dp", None, "tensor"), P(), P("tensor", None)),
        check_vma=False,
    )
```

```python
import functools

import jax
import jax.numpy as jnp
from jax import lax
from jax.experimental import pallas as pl
from jax.experimental.pallas import tpu as pltpu
from jax.sharding import PartitionSpec as P

F32, BF16 = jnp.float32, jnp.bfloat16
VMEM = pl.BlockSpec(memory_space=pltpu.VMEM)
HBM = pl.BlockSpec(memory_space=pltpu.HBM)
AXES = ("dp", "tensor")
LIMIT = 12 * 2**20
UNITS = 6
FIRST = 13


def split(x, terms):
    out = []
    for _ in range(terms):
        t = x.astype(BF16)
        out.append(t)
        x = x - t.astype(F32)
    return out


def stack(terms):
    return jnp.concatenate(terms, axis=0)


def dot(a, b, contract):
    return lax.dot_general(a, b, ((contract[:1], contract[1:]), ((), ())), preferred_element_type=F32)


def fold(x, rank):
    return functools.reduce(jnp.add, [x[i : i + rank] for i in range(0, x.shape[0], rank)])


def six_left(x):
    a, b, c = split(x, 3)
    return jnp.concatenate([a, a, b, a, b, c], axis=1)


def six_right(x):
    u, v, w = split(x, 3)
    return stack([u, v, u, w, v, u])


def walks(devices):
    bits = []
    bit = 2
    while bit < devices:
        bits.append(bit)
        bit *= 2
    walk = bits[::2] + bits[1::2]
    return walk, walk[1:] + walk[:1]


def role(place):
    return place.bit_count() & 1


def sides(devices):
    place = lax.axis_index("dp") * lax.axis_size("tensor") + lax.axis_index("tensor")
    half = 0
    for n in range(devices.bit_length() - 1):
        half = half ^ ((place >> n) & 1)
    first, second = ((place >> (walk[0].bit_length() - 1)) & 1 for walk in walks(devices))
    return (1 - half, jnp.where(half == 0, second, first)), (half, jnp.where(half == 0, first, second))


def start(pairs):
    for pair in pairs:
        for copy in pair:
            copy.start()


def wait(pairs):
    for pair in pairs:
        for copy in pair:
            copy.wait()


def left_kernel(q_hbm, g_hbm, e_hbm, m_ref, mh_ref, ml_ref, e_ref, g_ref, send_a, send_b, q_buf, g_buf, q_sem, sems, *, devices):
    theirs, mine = sides(devices)
    half = e_ref.shape[0]
    block = half // 2
    q_copy = pltpu.make_async_copy(q_hbm, q_buf, q_sem)
    q_copy.start()
    copies = []
    for n in range(4):
        source = pl.ds(pl.multiple_of((mine if n > 1 else theirs)[0] * half + n % 2 * block, block), block)
        to = pl.ds(n % 2 * block, block)
        copies.append(
            (
                pltpu.make_async_copy(g_hbm.at[source], (g_ref if n > 1 else g_buf).at[to], sems.at[n, 0]),
                pltpu.make_async_copy(e_hbm.at[source], (e_ref if n > 1 else m_ref).at[to], sems.at[n, 1]),
            )
        )
    start(copies[:3])
    q_copy.wait()
    q = stack(split(q_buf[...], 3))
    for n in range(2):
        wait(copies[n : n + 1])
        if n == 0:
            start(copies[3:])
        at = slice(n * block, (n + 1) * block)
        m = m_ref[at] + g_buf[at].astype(F32)
        m_ref[at] = m
        place(products(q, m, mh_ref, ml_ref, at), n * block, theirs[1], send_a, send_b)
    wait(copies[2:])


def left_rest_kernel(q_ref, e_ref, g_ref, m_ref, mh_ref, ml_ref, keep_a, keep_b, *, devices):
    _, (_, bit) = sides(devices)
    half = e_ref.shape[0]
    block = half // 2
    q = stack(split(q_ref[...], 3))
    for n in range(2):
        at = slice(n * block, (n + 1) * block)
        m = e_ref[at] + g_ref[at].astype(F32)
        m_ref[at] = m
        place(products(q, m, mh_ref, ml_ref, at), n * block, bit, keep_a, keep_b)


def place(p, start, bit, out_a, out_b):
    rows = out_b.shape[1]
    at = 0
    while at < p.shape[1]:
        unit, inside = (start + at) // rows, (start + at) % rows
        width = min(rows - inside, p.shape[1] - at)
        columns = slice(inside, inside + width)
        if unit == 2:
            out_b[:, columns] = p[:, at : at + width]
        else:
            out_a[1 - bit if unit == 0 else bit, :, columns] = p[:, at : at + width]
        at += width


def products(q, m, mh_ref, ml_ref, at):
    mh, ml = split(m, 2)
    mh_ref[at] = mh
    ml_ref[at] = ml
    return fold(dot(q, mh, (1, 1)) + dot(q, ml, (1, 1)), q.shape[0] // 3)


def square(p, rank):
    g = fold(dot(p, p, (1, 1)), rank)
    return g[:, :rank] + g[:, rank : 2 * rank] + g[:, 2 * rank :]


def terms_of(pieces):
    return jnp.concatenate([stack(split(x[...], 3)) for x in pieces], axis=1)


def unit_at(n, rows):
    return pl.ds(n * rows if isinstance(n, int) else pl.multiple_of(n * rows, rows), rows)


def right_early_kernel(a1, b0, a3, b1, a2, mh_ref, ml_ref, mh2_ref, ml2_ref, t_ref, gram_ref, *, devices):
    rank, rows = a1.shape
    (_, their_bit), (_, bit) = sides(devices)
    t = gram = 0.0
    for ref, unit, hs, ls in (
        (a3, bit, mh2_ref, ml2_ref),
        (b1, 2, mh2_ref, ml2_ref),
        (a1, their_bit, mh_ref, ml_ref),
        (b0, 2, mh_ref, ml_ref),
        (a2, 1 - bit, mh2_ref, ml2_ref),
    ):
        at = unit_at(unit, rows)
        p = terms_of((ref,))
        t = t + dot(p, hs[at], (1, 0)) + dot(p, ls[at], (1, 0))
        if ref is not a2:
            gram = gram + square(p, rank)
    t_ref[...] = fold(t, rank)
    gram_ref[...] = gram


def right_kernel(p_ref, mh_ref, ml_ref, before, t_ref, *, devices):
    rank, rows = p_ref.shape
    p = terms_of((p_ref,))
    at = unit_at(1 - sides(devices)[0][1], rows)
    t_ref[...] = before[...] + fold(dot(p, mh_ref[at], (1, 0)) + dot(p, ml_ref[at], (1, 0)), rank)


def eliminate(a, pivots):
    rank = a.shape[0]
    row = lax.broadcasted_iota(jnp.int32, (rank, 1), 0)
    for k in pivots:
        line = a[k : k + 1, :] / a[k : k + 1, k : k + 1]
        a = a - jnp.where(row > k, a[:, k : k + 1], 0.0) * line
    return a


def factor_kernel(gram_ref, a0, a2, state_ref):
    rank = gram_ref.shape[0]
    gram = gram_ref[...] + square(terms_of((a0, a2)), rank)
    row = lax.broadcasted_iota(jnp.int32, (rank, 128), 0)
    lane = lax.broadcasted_iota(jnp.int32, (rank, 128), 1)
    eye = (lane == row + rank).astype(F32)
    state_ref[...] = eliminate(jnp.concatenate([gram, eye[:, rank:]], axis=1), range(FIRST))


def inverse_kernel(state_ref, inv_ref):
    rank = state_ref.shape[0]
    a = eliminate(state_ref[...], range(FIRST, rank - 1))
    row = lax.broadcasted_iota(jnp.int32, a.shape, 0)
    lane = lax.broadcasted_iota(jnp.int32, a.shape, 1)
    pivots = jnp.sum(jnp.where(row == lane, a, 0.0), axis=1, keepdims=True)
    inv_ref[...] = a[:, rank : 2 * rank] / jnp.sqrt(pivots)


def hat_kernel(inv_ref, *refs, devices):
    pieces, (hat_hbm, rows_ref, hat_buf, sems) = refs[:UNITS], refs[UNITS:]
    rows = pieces[0].shape[1]
    inverse = inv_ref[...]
    left, back = six_left(inverse), six_left(inverse.T)
    copies, units = [], []
    for n, (core, bit) in enumerate(sides(devices)):
        for k, unit in enumerate((1 - bit, bit, 2)):
            i = 3 * n + k
            units.append(3 * n + unit)
            at = pl.ds(i * rows, rows)
            hat_buf[:, at] = dot(left, six_right(pieces[i][...]), (1, 0))
            copies.append(pltpu.make_async_copy(hat_buf.at[:, at], hat_hbm.at[:, unit_at(3 * core + unit, rows)], sems.at[i]))
            copies[-1].start()
    for i in range(UNITS):
        u, v = split(dot(back, six_right(hat_buf[:, i * rows : (i + 1) * rows]), (1, 0)), 2)
        rows_ref[unit_at(units[i], rows), :] = stack([u, v, u, v]).T
    for copy in copies:
        copy.wait()


def error_kernel(t0_ref, t1_ref, inv_ref, rows_ref, m_ref, m2_ref, out_hbm, q_hbm, buf, q_buf, sems, q_sem, *, replicas, cuts, devices):
    t = (t0_ref[...] + t1_ref[...]) / replicas
    u, v = split(t, 2)
    terms = stack([u, u, v, v])
    half = m_ref.shape[0]
    copies = []
    for source, side, shift in ((m_ref, 0, 0), (m2_ref, 1, half)):
        for at, end in zip(cuts[:-1], cuts[1:], strict=True):
            here = slice(shift + at, shift + end)
            buf[here] = source[at:end] - dot(rows_ref[here], terms, (1, 0))
            to = pl.ds(pl.multiple_of(sides(devices)[side][0] * half + at, 16), end - at)
            copies.append(pltpu.make_async_copy(buf.at[pl.ds(shift + at, end - at)], out_hbm.at[to], sems.at[len(copies)]))
            copies[-1].start()
    q_buf[...] = dot(six_left(inv_ref[...]), six_right(t), (1, 0))
    copies.append(pltpu.make_async_copy(q_buf, q_hbm, q_sem))
    copies[-1].start()
    for copy in copies:
        copy.wait()


def shards(gradient, error_buffer, q_given):
    replicas, tensors = lax.axis_size("dp"), lax.axis_size("tensor")
    devices = replicas * tensors
    depth, columns = gradient.shape[1:]
    rank = q_given.shape[1]
    rows = depth // UNITS

    def call(kernel, name, flops, **kw):
        made = pl.pallas_call(
            kernel,
            name=name,
            compiler_params=pltpu.CompilerParams(vmem_limit_bytes=LIMIT),
            cost_estimate=pl.CostEstimate(flops=flops, bytes_accessed=0, transcendentals=0),
            **kw,
        )
        spaces = [pltpu.HBM if spec is HBM else pltpu.VMEM for spec in kw["in_specs"]]
        return lambda *args: made(*(pltpu.with_memory_space_constraint(x, space) for x, space in zip(args, spaces, strict=True)))

    unit = pltpu.VMEM((rank, rows), F32)
    small = pltpu.VMEM((rank, rank), F32)
    wide = pltpu.VMEM((rank, columns), F32)
    work = 6 * depth * columns * rank

    merged = tuple(pltpu.VMEM((depth // 2, columns), kind) for kind in (F32, BF16, BF16))
    two = pltpu.VMEM((2, rank, rows), F32)
    m, mh, ml, e_own, g_own, send_a, send_b = call(
        functools.partial(left_kernel, devices=devices),
        "left_products",
        work,
        out_shape=merged + merged[:2] + (two, unit),
        in_specs=[HBM] * 3,
        out_specs=(VMEM,) * 7,
        scratch_shapes=[
            pltpu.VMEM((rank, columns), F32),
            pltpu.VMEM((depth // 2, columns), BF16),
            pltpu.SemaphoreType.DMA(()),
            pltpu.SemaphoreType.DMA((4, 2)),
        ],
    )(q_given.T, gradient[0], error_buffer[0])
    m2, mh2, ml2, keep_a, keep_b = call(
        functools.partial(left_rest_kernel, devices=devices),
        "left_products_rest",
        work,
        out_shape=merged + (two, unit),
        in_specs=[VMEM] * 3,
        out_specs=(VMEM,) * 5,
    )(q_given.T, e_own, g_own)

    def swap(x, bit):
        return lax.ppermute(x, AXES, [(i, i ^ bit) for i in range(devices)])

    def cross(x, *bits):
        return lax.ppermute(x, AXES, [(i, i ^ 1 ^ bits[role(i)]) for i in range(devices)])

    walk = list(zip(*walks(devices), strict=True))
    both = keep_a + swap(send_a, 1)
    b1 = keep_b + swap(send_b, 1)
    sent, a3 = both[0], both[1]
    for n, bits in enumerate(walk):
        arrived = cross(sent if n == 0 else a3, *bits), cross(b1, *bits)
        a3, b1 = a3 + arrived[0], b1 + arrived[1]
    a2 = cross(a3, *walk[0])
    a1, b0, a0 = swap(a3, 1), swap(b1, 1), swap(a2, 1)

    t, gram = call(
        functools.partial(right_early_kernel, devices=devices),
        "right_products",
        work,
        out_shape=(wide, small),
        in_specs=[VMEM] * 9,
        out_specs=(VMEM, VMEM),
    )(a1, b0, a3, b1, a2, mh, ml, mh2, ml2)
    t = call(
        functools.partial(right_kernel, devices=devices),
        "right_products_last",
        work,
        out_shape=wide,
        in_specs=[VMEM] * 4,
        out_specs=VMEM,
    )(a0, mh, ml, t)

    state = call(
        factor_kernel,
        "factor_first_half",
        work,
        out_shape=pltpu.VMEM((rank, 128), F32),
        in_specs=[VMEM] * 3,
        out_specs=VMEM,
    )(gram, a0, a2)
    inverse = call(inverse_kernel, "factor_second_half", work, out_shape=small, in_specs=[VMEM], out_specs=VMEM)(state)
    hat, hat_rows = call(
        functools.partial(hat_kernel, devices=devices),
        "left_factor",
        work,
        out_shape=(pltpu.HBM((rank, depth), F32), pltpu.VMEM((depth, 4 * rank), BF16)),
        in_specs=[VMEM] * (1 + UNITS),
        out_specs=(HBM, VMEM),
        scratch_shapes=[pltpu.VMEM((rank, depth), F32), pltpu.SemaphoreType.DMA((UNITS,))],
    )(inverse, a0, a1, b0, a2, a3, b1)

    bits = sorted(bit for bit in walks(devices)[0] if bit >= tensors)
    turns = len(bits) // 2 * 2
    beside = [state, inverse]
    parts = t, None
    for n, bit in enumerate(bits):
        if n:
            t = parts[0] + parts[1]
            if n <= len(beside):
                t, _ = lax.optimization_barrier((t, beside[n - 1]))
        parts = (swap(t, 1), swap(t, 1 ^ bit)) if n < turns else (t, swap(t, bit))

    half = depth // 2
    cuts = [half * n // 18 // 16 * 16 for n in (0, 1, 3, 6, 10, 14, 18)]
    error, q_new = call(
        functools.partial(error_kernel, replicas=replicas, cuts=cuts, devices=devices),
        "new_error",
        work,
        out_shape=(pltpu.HBM((depth, columns), F32), pltpu.HBM((rank, columns), F32)),
        in_specs=[VMEM] * 6,
        out_specs=(HBM, HBM),
        scratch_shapes=[
            pltpu.VMEM((depth, columns), F32),
            pltpu.VMEM((rank, columns), F32),
            pltpu.SemaphoreType.DMA((2 * len(cuts) - 2,)),
            pltpu.SemaphoreType.DMA(()),
        ],
    )(*parts, inverse, hat_rows, m, m2)
    return (error[None], hat.T, q_new.T)


def solution(mesh):
    placed = (P("dp", None, "tensor"), P("dp", None, "tensor"), P("tensor", None))
    return jax.shard_map(
        shards,
        mesh=mesh,
        in_specs=placed,
        out_specs=(P("dp", None, "tensor"), P(), P("tensor", None)),
        check_vma=False,
    )
```

```python
import functools

import jax
import jax.numpy as jnp
from jax import lax
from jax.experimental import pallas as pl
from jax.experimental.pallas import tpu as pltpu
from jax.sharding import PartitionSpec as P

F32, BF16 = jnp.float32, jnp.bfloat16
VMEM = pl.BlockSpec(memory_space=pltpu.VMEM)
HBM = pl.BlockSpec(memory_space=pltpu.HBM)
AXES = ("dp", "tensor")
LIMIT = 12 * 2**20
UNITS = 6
FIRST = 13


def split(x, terms):
    out = []
    for _ in range(terms):
        t = x.astype(BF16)
        out.append(t)
        x = x - t.astype(F32)
    return out


def stack(terms):
    return jnp.concatenate(terms, axis=0)


def dot(a, b, contract):
    return lax.dot_general(a, b, ((contract[:1], contract[1:]), ((), ())), preferred_element_type=F32)


def fold(x, rank):
    return functools.reduce(jnp.add, [x[i : i + rank] for i in range(0, x.shape[0], rank)])


def six_left(x):
    a, b, c = split(x, 3)
    return jnp.concatenate([a, a, b, a, b, c], axis=1)


def six_right(x):
    u, v, w = split(x, 3)
    return stack([u, v, u, w, v, u])


def walks(devices):
    bits = []
    bit = 2
    while bit < devices:
        bits.append(bit)
        bit *= 2
    walk = bits[::2] + bits[1::2]
    return walk, walk[1:] + walk[:1]


def role(place):
    return place.bit_count() & 1


def sides(devices):
    place = lax.axis_index("dp") * lax.axis_size("tensor") + lax.axis_index("tensor")
    half = 0
    for n in range(devices.bit_length() - 1):
        half = half ^ ((place >> n) & 1)
    first, second = ((place >> (walk[0].bit_length() - 1)) & 1 for walk in walks(devices))
    return (1 - half, jnp.where(half == 0, second, first)), (half, jnp.where(half == 0, first, second))


def start(pairs):
    for pair in pairs:
        for copy in pair:
            copy.start()


def wait(pairs):
    for pair in pairs:
        for copy in pair:
            copy.wait()


def left_kernel(q_hbm, g_hbm, e_hbm, m_ref, mh_ref, ml_ref, e_ref, g_ref, send_a, send_b, q_buf, g_buf, q_sem, sems, *, devices):
    theirs, mine = sides(devices)
    half = e_ref.shape[0]
    block = half // 2
    q_copy = pltpu.make_async_copy(q_hbm, q_buf, q_sem)
    q_copy.start()
    copies = []
    for n in range(4):
        source = pl.ds(pl.multiple_of((mine if n > 1 else theirs)[0] * half + n % 2 * block, block), block)
        to = pl.ds(n % 2 * block, block)
        copies.append(
            (
                pltpu.make_async_copy(g_hbm.at[source], (g_ref if n > 1 else g_buf).at[to], sems.at[n, 0]),
                pltpu.make_async_copy(e_hbm.at[source], (e_ref if n > 1 else m_ref).at[to], sems.at[n, 1]),
            )
        )
    start(copies[:3])
    q_copy.wait()
    q = stack(split(q_buf[...], 3))
    for n in range(2):
        wait(copies[n : n + 1])
        if n == 0:
            start(copies[3:])
        at = slice(n * block, (n + 1) * block)
        m = m_ref[at] + g_buf[at].astype(F32)
        m_ref[at] = m
        place(products(q, m, mh_ref, ml_ref, at), n * block, theirs[1], send_a, send_b)
    wait(copies[2:])


def left_rest_kernel(q_ref, e_ref, g_ref, m_ref, mh_ref, ml_ref, keep_a, keep_b, *, devices):
    _, (_, bit) = sides(devices)
    half = e_ref.shape[0]
    block = half // 2
    q = stack(split(q_ref[...], 3))
    for n in range(2):
        at = slice(n * block, (n + 1) * block)
        m = e_ref[at] + g_ref[at].astype(F32)
        m_ref[at] = m
        place(products(q, m, mh_ref, ml_ref, at), n * block, bit, keep_a, keep_b)


def place(p, start, bit, out_a, out_b):
    rows = out_b.shape[1]
    at = 0
    while at < p.shape[1]:
        unit, inside = (start + at) // rows, (start + at) % rows
        width = min(rows - inside, p.shape[1] - at)
        columns = slice(inside, inside + width)
        if unit == 2:
            out_b[:, columns] = p[:, at : at + width]
        else:
            out_a[1 - bit if unit == 0 else bit, :, columns] = p[:, at : at + width]
        at += width


def products(q, m, mh_ref, ml_ref, at):
    mh, ml = split(m, 2)
    mh_ref[at] = mh
    ml_ref[at] = ml
    return fold(dot(q, mh, (1, 1)) + dot(q, ml, (1, 1)), q.shape[0] // 3)


def square(p, rank):
    g = fold(dot(p, p, (1, 1)), rank)
    return g[:, :rank] + g[:, rank : 2 * rank] + g[:, 2 * rank :]


def terms_of(pieces):
    return jnp.concatenate([stack(split(x[...], 3)) for x in pieces], axis=1)


def unit_at(n, rows):
    return pl.ds(n * rows if isinstance(n, int) else pl.multiple_of(n * rows, rows), rows)


def right_early_kernel(a1, b0, a3, b1, a2, mh_ref, ml_ref, mh2_ref, ml2_ref, t_ref, *, devices):
    rank, rows = a1.shape
    (_, their_bit), (_, bit) = sides(devices)
    t = 0.0
    for ref, unit, hs, ls in (
        (a3, bit, mh2_ref, ml2_ref),
        (b1, 2, mh2_ref, ml2_ref),
        (a1, their_bit, mh_ref, ml_ref),
        (b0, 2, mh_ref, ml_ref),
        (a2, 1 - bit, mh2_ref, ml2_ref),
    ):
        at = unit_at(unit, rows)
        p = terms_of((ref,))
        t = t + dot(p, hs[at], (1, 0)) + dot(p, ls[at], (1, 0))
    t_ref[...] = fold(t, rank)


def right_kernel(p_ref, mh_ref, ml_ref, before, t_ref, *, devices):
    rank, rows = p_ref.shape
    p = terms_of((p_ref,))
    at = unit_at(1 - sides(devices)[0][1], rows)
    t_ref[...] = before[...] + fold(dot(p, mh_ref[at], (1, 0)) + dot(p, ml_ref[at], (1, 0)), rank)


def eliminate(a, pivots):
    rank = a.shape[0]
    row = lax.broadcasted_iota(jnp.int32, (rank, 1), 0)
    for k in pivots:
        line = a[k : k + 1, :] / a[k : k + 1, k : k + 1]
        a = a - jnp.where(row > k, a[:, k : k + 1], 0.0) * line
    return a


def factor_kernel(*refs):
    pieces, state_ref = refs[:UNITS], refs[UNITS]
    rank = pieces[0].shape[0]
    gram = square(terms_of(pieces), rank)
    row = lax.broadcasted_iota(jnp.int32, (rank, 128), 0)
    lane = lax.broadcasted_iota(jnp.int32, (rank, 128), 1)
    eye = (lane == row + rank).astype(F32)
    state_ref[...] = eliminate(jnp.concatenate([gram, eye[:, rank:]], axis=1), range(FIRST))


def inverse_kernel(state_ref, inv_ref):
    rank = state_ref.shape[0]
    a = eliminate(state_ref[...], range(FIRST, rank - 1))
    row = lax.broadcasted_iota(jnp.int32, a.shape, 0)
    lane = lax.broadcasted_iota(jnp.int32, a.shape, 1)
    pivots = jnp.sum(jnp.where(row == lane, a, 0.0), axis=1, keepdims=True)
    inv_ref[...] = a[:, rank : 2 * rank] / jnp.sqrt(pivots)


def hat_kernel(inv_ref, *refs, devices):
    pieces, (hat_hbm, rows_ref, hat_buf, sems) = refs[:UNITS], refs[UNITS:]
    rows = pieces[0].shape[1]
    inverse = inv_ref[...]
    left, back = six_left(inverse), six_left(inverse.T)
    copies, units = [], []
    for n, (core, bit) in enumerate(sides(devices)):
        for k, unit in enumerate((1 - bit, bit, 2)):
            i = 3 * n + k
            units.append(3 * n + unit)
            at = pl.ds(i * rows, rows)
            hat_buf[:, at] = dot(left, six_right(pieces[i][...]), (1, 0))
            copies.append(pltpu.make_async_copy(hat_buf.at[:, at], hat_hbm.at[:, unit_at(3 * core + unit, rows)], sems.at[i]))
            copies[-1].start()
    for i in range(UNITS):
        u, v = split(dot(back, six_right(hat_buf[:, i * rows : (i + 1) * rows]), (1, 0)), 2)
        rows_ref[unit_at(units[i], rows), :] = stack([u, v, u, v]).T
    for copy in copies:
        copy.wait()


def error_kernel(t0_ref, t1_ref, inv_ref, rows_ref, m_ref, m2_ref, out_hbm, q_hbm, buf, q_buf, sems, q_sem, *, replicas, cuts, devices):
    t = (t0_ref[...] + t1_ref[...]) / replicas
    u, v = split(t, 2)
    terms = stack([u, u, v, v])
    half = m_ref.shape[0]
    copies = []
    for source, side, shift in ((m_ref, 0, 0), (m2_ref, 1, half)):
        for at, end in zip(cuts[:-1], cuts[1:], strict=True):
            here = slice(shift + at, shift + end)
            buf[here] = source[at:end] - dot(rows_ref[here], terms, (1, 0))
            to = pl.ds(pl.multiple_of(sides(devices)[side][0] * half + at, 16), end - at)
            copies.append(pltpu.make_async_copy(buf.at[pl.ds(shift + at, end - at)], out_hbm.at[to], sems.at[len(copies)]))
            copies[-1].start()
    q_buf[...] = dot(six_left(inv_ref[...]), six_right(t), (1, 0))
    copies.append(pltpu.make_async_copy(q_buf, q_hbm, q_sem))
    copies[-1].start()
    for copy in copies:
        copy.wait()


def shards(gradient, error_buffer, q_given):
    replicas, tensors = lax.axis_size("dp"), lax.axis_size("tensor")
    devices = replicas * tensors
    depth, columns = gradient.shape[1:]
    rank = q_given.shape[1]
    rows = depth // UNITS

    def call(kernel, name, flops, **kw):
        made = pl.pallas_call(
            kernel,
            name=name,
            compiler_params=pltpu.CompilerParams(vmem_limit_bytes=LIMIT),
            cost_estimate=pl.CostEstimate(flops=flops, bytes_accessed=0, transcendentals=0),
            **kw,
        )
        spaces = [pltpu.HBM if spec is HBM else pltpu.VMEM for spec in kw["in_specs"]]
        return lambda *args: made(*(pltpu.with_memory_space_constraint(x, space) for x, space in zip(args, spaces, strict=True)))

    unit = pltpu.VMEM((rank, rows), F32)
    small = pltpu.VMEM((rank, rank), F32)
    wide = pltpu.VMEM((rank, columns), F32)
    work = 6 * depth * columns * rank

    merged = tuple(pltpu.VMEM((depth // 2, columns), kind) for kind in (F32, BF16, BF16))
    two = pltpu.VMEM((2, rank, rows), F32)
    m, mh, ml, e_own, g_own, send_a, send_b = call(
        functools.partial(left_kernel, devices=devices),
        "left_products",
        work,
        out_shape=merged + merged[:2] + (two, unit),
        in_specs=[HBM] * 3,
        out_specs=(VMEM,) * 7,
        scratch_shapes=[
            pltpu.VMEM((rank, columns), F32),
            pltpu.VMEM((depth // 2, columns), BF16),
            pltpu.SemaphoreType.DMA(()),
            pltpu.SemaphoreType.DMA((4, 2)),
        ],
    )(q_given.T, gradient[0], error_buffer[0])
    m2, mh2, ml2, keep_a, keep_b = call(
        functools.partial(left_rest_kernel, devices=devices),
        "left_products_rest",
        work,
        out_shape=merged + (two, unit),
        in_specs=[VMEM] * 3,
        out_specs=(VMEM,) * 5,
    )(q_given.T, e_own, g_own)

    def swap(x, bit):
        return lax.ppermute(x, AXES, [(i, i ^ bit) for i in range(devices)])

    def cross(x, *bits):
        return lax.ppermute(x, AXES, [(i, i ^ 1 ^ bits[role(i)]) for i in range(devices)])

    walk = list(zip(*walks(devices), strict=True))
    both = keep_a + swap(send_a, 1)
    b1 = keep_b + swap(send_b, 1)
    sent, a3 = both[0], both[1]
    for n, bits in enumerate(walk):
        arrived = cross(sent if n == 0 else a3, *bits), cross(b1, *bits)
        a3, b1 = a3 + arrived[0], b1 + arrived[1]
    a2 = cross(a3, *walk[0])
    a1, b0, a0 = swap(a3, 1), swap(b1, 1), swap(a2, 1)

    t = call(
        functools.partial(right_early_kernel, devices=devices),
        "right_products",
        work,
        out_shape=wide,
        in_specs=[VMEM] * 9,
        out_specs=VMEM,
    )(a1, b0, a3, b1, a2, mh, ml, mh2, ml2)
    t = call(
        functools.partial(right_kernel, devices=devices),
        "right_products_last",
        work,
        out_shape=wide,
        in_specs=[VMEM] * 4,
        out_specs=VMEM,
    )(a0, mh, ml, t)

    state = call(
        factor_kernel,
        "factor_first_half",
        work,
        out_shape=pltpu.VMEM((rank, 128), F32),
        in_specs=[VMEM] * UNITS,
        out_specs=VMEM,
    )(a0, a1, b0, a2, a3, b1)
    inverse = call(inverse_kernel, "factor_second_half", work, out_shape=small, in_specs=[VMEM], out_specs=VMEM)(state)
    hat, hat_rows = call(
        functools.partial(hat_kernel, devices=devices),
        "left_factor",
        work,
        out_shape=(pltpu.HBM((rank, depth), F32), pltpu.VMEM((depth, 4 * rank), BF16)),
        in_specs=[VMEM] * (1 + UNITS),
        out_specs=(HBM, VMEM),
        scratch_shapes=[pltpu.VMEM((rank, depth), F32), pltpu.SemaphoreType.DMA((UNITS,))],
    )(inverse, a0, a1, b0, a2, a3, b1)

    bits = sorted(bit for bit in walks(devices)[0] if bit >= tensors)
    turns = len(bits) // 2 * 2
    beside = [state, inverse]
    parts = t, None
    for n, bit in enumerate(bits):
        if n:
            t = parts[0] + parts[1]
            if n <= len(beside):
                t, _ = lax.optimization_barrier((t, beside[n - 1]))
        parts = (swap(t, 1), swap(t, 1 ^ bit)) if n < turns else (t, swap(t, bit))

    half = depth // 2
    cuts = [half * n // 18 // 16 * 16 for n in (0, 1, 3, 6, 10, 14, 18)]
    error, q_new = call(
        functools.partial(error_kernel, replicas=replicas, cuts=cuts, devices=devices),
        "new_error",
        work,
        out_shape=(pltpu.HBM((depth, columns), F32), pltpu.HBM((rank, columns), F32)),
        in_specs=[VMEM] * 6,
        out_specs=(HBM, HBM),
        scratch_shapes=[
            pltpu.VMEM((depth, columns), F32),
            pltpu.VMEM((rank, columns), F32),
            pltpu.SemaphoreType.DMA((2 * len(cuts) - 2,)),
            pltpu.SemaphoreType.DMA(()),
        ],
    )(*parts, inverse, hat_rows, m, m2)
    return (error[None], hat.T, q_new.T)


def solution(mesh):
    placed = (P("dp", None, "tensor"), P("dp", None, "tensor"), P("tensor", None))
    return jax.shard_map(
        shards,
        mesh=mesh,
        in_specs=placed,
        out_specs=(P("dp", None, "tensor"), P(), P("tensor", None)),
        check_vma=False,
    )
```

```python
import functools

import jax
import jax.numpy as jnp
from jax import lax
from jax.experimental import pallas as pl
from jax.experimental.pallas import tpu as pltpu
from jax.sharding import PartitionSpec as P

F32, BF16 = jnp.float32, jnp.bfloat16
VMEM = pl.BlockSpec(memory_space=pltpu.VMEM)
HBM = pl.BlockSpec(memory_space=pltpu.HBM)
AXES = ("dp", "tensor")
LIMIT = 12 * 2**20
UNITS = 6
FIRST = 13


def split(x, terms):
    out = []
    for _ in range(terms):
        t = x.astype(BF16)
        out.append(t)
        x = x - t.astype(F32)
    return out


def stack(terms):
    return jnp.concatenate(terms, axis=0)


def dot(a, b, contract):
    return lax.dot_general(a, b, ((contract[:1], contract[1:]), ((), ())), preferred_element_type=F32)


def fold(x, rank):
    return functools.reduce(jnp.add, [x[i : i + rank] for i in range(0, x.shape[0], rank)])


def six_left(x):
    a, b, c = split(x, 3)
    return jnp.concatenate([a, a, b, a, b, c], axis=1)


def six_right(x):
    u, v, w = split(x, 3)
    return stack([u, v, u, w, v, u])


def walks(devices):
    bits = []
    bit = 2
    while bit < devices:
        bits.append(bit)
        bit *= 2
    walk = bits[::2] + bits[1::2]
    return walk, walk[1:] + walk[:1]


def role(place):
    return place.bit_count() & 1


def sides(devices):
    place = lax.axis_index("dp") * lax.axis_size("tensor") + lax.axis_index("tensor")
    half = 0
    for n in range(devices.bit_length() - 1):
        half = half ^ ((place >> n) & 1)
    first, second = ((place >> (walk[0].bit_length() - 1)) & 1 for walk in walks(devices))
    return (1 - half, jnp.where(half == 0, second, first)), (half, jnp.where(half == 0, first, second))


def start(pairs):
    for pair in pairs:
        for copy in pair:
            copy.start()


def wait(pairs):
    for pair in pairs:
        for copy in pair:
            copy.wait()


def left_kernel(q_hbm, g_hbm, e_hbm, m_ref, mh_ref, ml_ref, e_ref, g_ref, send_a, send_b, q_buf, g_buf, q_sem, sems, *, devices):
    theirs, mine = sides(devices)
    half = e_ref.shape[0]
    block = half // 2
    q_copy = pltpu.make_async_copy(q_hbm, q_buf, q_sem)
    q_copy.start()
    copies = []
    for n in range(4):
        source = pl.ds(pl.multiple_of((mine if n > 1 else theirs)[0] * half + n % 2 * block, block), block)
        to = pl.ds(n % 2 * block, block)
        copies.append(
            (
                pltpu.make_async_copy(e_hbm.at[source], (e_ref if n > 1 else m_ref).at[to], sems.at[n, 1]),
                pltpu.make_async_copy(g_hbm.at[source], (g_ref if n > 1 else g_buf).at[to], sems.at[n, 0]),
            )
        )
    start(copies[:3])
    q_copy.wait()
    q = stack(split(q_buf[...], 3))
    for n in range(2):
        wait(copies[n : n + 1])
        if n == 0:
            start(copies[3:])
        at = slice(n * block, (n + 1) * block)
        m = m_ref[at] + g_buf[at].astype(F32)
        m_ref[at] = m
        place(products(q, m, mh_ref, ml_ref, at), n * block, theirs[1], send_a, send_b)
    wait(copies[2:])


def left_rest_kernel(q_ref, e_ref, g_ref, m_ref, mh_ref, ml_ref, keep_a, keep_b, *, devices):
    _, (_, bit) = sides(devices)
    half = e_ref.shape[0]
    block = half // 2
    q = stack(split(q_ref[...], 3))
    for n in range(2):
        at = slice(n * block, (n + 1) * block)
        m = e_ref[at] + g_ref[at].astype(F32)
        m_ref[at] = m
        place(products(q, m, mh_ref, ml_ref, at), n * block, bit, keep_a, keep_b)


def place(p, start, bit, out_a, out_b):
    rows = out_b.shape[1]
    at = 0
    while at < p.shape[1]:
        unit, inside = (start + at) // rows, (start + at) % rows
        width = min(rows - inside, p.shape[1] - at)
        columns = slice(inside, inside + width)
        if unit == 2:
            out_b[:, columns] = p[:, at : at + width]
        else:
            out_a[1 - bit if unit == 0 else bit, :, columns] = p[:, at : at + width]
        at += width


def products(q, m, mh_ref, ml_ref, at):
    mh, ml = split(m, 2)
    mh_ref[at] = mh
    ml_ref[at] = ml
    return fold(dot(q, mh, (1, 1)) + dot(q, ml, (1, 1)), q.shape[0] // 3)


def square(p, rank):
    g = fold(dot(p, p, (1, 1)), rank)
    return g[:, :rank] + g[:, rank : 2 * rank] + g[:, 2 * rank :]


def terms_of(pieces):
    return jnp.concatenate([stack(split(x[...], 3)) for x in pieces], axis=1)


def unit_at(n, rows):
    return pl.ds(n * rows if isinstance(n, int) else pl.multiple_of(n * rows, rows), rows)


def right_early_kernel(a1, b0, a3, b1, a2, mh_ref, ml_ref, mh2_ref, ml2_ref, t_ref, *, devices):
    rank, rows = a1.shape
    (_, their_bit), (_, bit) = sides(devices)
    t = 0.0
    for ref, unit, hs, ls in (
        (a3, bit, mh2_ref, ml2_ref),
        (b1, 2, mh2_ref, ml2_ref),
        (a1, their_bit, mh_ref, ml_ref),
        (b0, 2, mh_ref, ml_ref),
        (a2, 1 - bit, mh2_ref, ml2_ref),
    ):
        at = unit_at(unit, rows)
        p = terms_of((ref,))
        t = t + dot(p, hs[at], (1, 0)) + dot(p, ls[at], (1, 0))
    t_ref[...] = fold(t, rank)


def right_kernel(p_ref, mh_ref, ml_ref, before, t_ref, *, devices):
    rank, rows = p_ref.shape
    p = terms_of((p_ref,))
    at = unit_at(1 - sides(devices)[0][1], rows)
    t_ref[...] = before[...] + fold(dot(p, mh_ref[at], (1, 0)) + dot(p, ml_ref[at], (1, 0)), rank)


def eliminate(a, pivots):
    rank = a.shape[0]
    row = lax.broadcasted_iota(jnp.int32, (rank, 1), 0)
    for k in pivots:
        line = a[k : k + 1, :] / a[k : k + 1, k : k + 1]
        a = a - jnp.where(row > k, a[:, k : k + 1], 0.0) * line
    return a


def factor_kernel(*refs):
    pieces, state_ref = refs[:UNITS], refs[UNITS]
    rank = pieces[0].shape[0]
    gram = square(terms_of(pieces), rank)
    row = lax.broadcasted_iota(jnp.int32, (rank, 128), 0)
    lane = lax.broadcasted_iota(jnp.int32, (rank, 128), 1)
    eye = (lane == row + rank).astype(F32)
    state_ref[...] = eliminate(jnp.concatenate([gram, eye[:, rank:]], axis=1), range(FIRST))


def inverse_kernel(state_ref, inv_ref):
    rank = state_ref.shape[0]
    a = eliminate(state_ref[...], range(FIRST, rank - 1))
    row = lax.broadcasted_iota(jnp.int32, a.shape, 0)
    lane = lax.broadcasted_iota(jnp.int32, a.shape, 1)
    pivots = jnp.sum(jnp.where(row == lane, a, 0.0), axis=1, keepdims=True)
    inv_ref[...] = a[:, rank : 2 * rank] / jnp.sqrt(pivots)


def hat_kernel(inv_ref, *refs, devices):
    pieces, (hat_hbm, rows_ref, hat_buf, sems) = refs[:UNITS], refs[UNITS:]
    rows = pieces[0].shape[1]
    inverse = inv_ref[...]
    left, back = six_left(inverse), six_left(inverse.T)
    copies, units = [], []
    for n, (core, bit) in enumerate(sides(devices)):
        for k, unit in enumerate((1 - bit, bit, 2)):
            i = 3 * n + k
            units.append(3 * n + unit)
            at = pl.ds(i * rows, rows)
            hat_buf[:, at] = dot(left, six_right(pieces[i][...]), (1, 0))
            copies.append(pltpu.make_async_copy(hat_buf.at[:, at], hat_hbm.at[:, unit_at(3 * core + unit, rows)], sems.at[i]))
            copies[-1].start()
    for i in range(UNITS):
        u, v = split(dot(back, six_right(hat_buf[:, i * rows : (i + 1) * rows]), (1, 0)), 2)
        rows_ref[unit_at(units[i], rows), :] = stack([u, v, u, v]).T
    for copy in copies:
        copy.wait()


def error_kernel(t0_ref, t1_ref, inv_ref, rows_ref, m_ref, m2_ref, out_hbm, q_hbm, buf, q_buf, sems, q_sem, *, replicas, cuts, devices):
    t = (t0_ref[...] + t1_ref[...]) / replicas
    u, v = split(t, 2)
    terms = stack([u, u, v, v])
    half = m_ref.shape[0]
    copies = []
    for source, side, shift in ((m_ref, 0, 0), (m2_ref, 1, half)):
        for at, end in zip(cuts[:-1], cuts[1:], strict=True):
            here = slice(shift + at, shift + end)
            buf[here] = source[at:end] - dot(rows_ref[here], terms, (1, 0))
            to = pl.ds(pl.multiple_of(sides(devices)[side][0] * half + at, 16), end - at)
            copies.append(pltpu.make_async_copy(buf.at[pl.ds(shift + at, end - at)], out_hbm.at[to], sems.at[len(copies)]))
            copies[-1].start()
    q_buf[...] = dot(six_left(inv_ref[...]), six_right(t), (1, 0))
    copies.append(pltpu.make_async_copy(q_buf, q_hbm, q_sem))
    copies[-1].start()
    for copy in copies:
        copy.wait()


def shards(gradient, error_buffer, q_given):
    replicas, tensors = lax.axis_size("dp"), lax.axis_size("tensor")
    devices = replicas * tensors
    depth, columns = gradient.shape[1:]
    rank = q_given.shape[1]
    rows = depth // UNITS

    def call(kernel, name, flops, **kw):
        made = pl.pallas_call(
            kernel,
            name=name,
            compiler_params=pltpu.CompilerParams(vmem_limit_bytes=LIMIT),
            cost_estimate=pl.CostEstimate(flops=flops, bytes_accessed=0, transcendentals=0),
            **kw,
        )
        spaces = [pltpu.HBM if spec is HBM else pltpu.VMEM for spec in kw["in_specs"]]
        return lambda *args: made(*(pltpu.with_memory_space_constraint(x, space) for x, space in zip(args, spaces, strict=True)))

    unit = pltpu.VMEM((rank, rows), F32)
    small = pltpu.VMEM((rank, rank), F32)
    wide = pltpu.VMEM((rank, columns), F32)
    work = 6 * depth * columns * rank

    merged = tuple(pltpu.VMEM((depth // 2, columns), kind) for kind in (F32, BF16, BF16))
    two = pltpu.VMEM((2, rank, rows), F32)
    m, mh, ml, e_own, g_own, send_a, send_b = call(
        functools.partial(left_kernel, devices=devices),
        "left_products",
        work,
        out_shape=merged + merged[:2] + (two, unit),
        in_specs=[HBM] * 3,
        out_specs=(VMEM,) * 7,
        scratch_shapes=[
            pltpu.VMEM((rank, columns), F32),
            pltpu.VMEM((depth // 2, columns), BF16),
            pltpu.SemaphoreType.DMA(()),
            pltpu.SemaphoreType.DMA((4, 2)),
        ],
    )(q_given.T, gradient[0], error_buffer[0])
    m2, mh2, ml2, keep_a, keep_b = call(
        functools.partial(left_rest_kernel, devices=devices),
        "left_products_rest",
        work,
        out_shape=merged + (two, unit),
        in_specs=[VMEM] * 3,
        out_specs=(VMEM,) * 5,
    )(q_given.T, e_own, g_own)

    def swap(x, bit):
        return lax.ppermute(x, AXES, [(i, i ^ bit) for i in range(devices)])

    def cross(x, *bits):
        return lax.ppermute(x, AXES, [(i, i ^ 1 ^ bits[role(i)]) for i in range(devices)])

    walk = list(zip(*walks(devices), strict=True))
    both = keep_a + swap(send_a, 1)
    b1 = keep_b + swap(send_b, 1)
    sent, a3 = both[0], both[1]
    for n, bits in enumerate(walk):
        arrived = cross(sent if n == 0 else a3, *bits), cross(b1, *bits)
        a3, b1 = a3 + arrived[0], b1 + arrived[1]
    a2 = cross(a3, *walk[0])
    a1, b0, a0 = swap(a3, 1), swap(b1, 1), swap(a2, 1)

    t = call(
        functools.partial(right_early_kernel, devices=devices),
        "right_products",
        work,
        out_shape=wide,
        in_specs=[VMEM] * 9,
        out_specs=VMEM,
    )(a1, b0, a3, b1, a2, mh, ml, mh2, ml2)
    t = call(
        functools.partial(right_kernel, devices=devices),
        "right_products_last",
        work,
        out_shape=wide,
        in_specs=[VMEM] * 4,
        out_specs=VMEM,
    )(a0, mh, ml, t)

    state = call(
        factor_kernel,
        "factor_first_half",
        work,
        out_shape=pltpu.VMEM((rank, 128), F32),
        in_specs=[VMEM] * UNITS,
        out_specs=VMEM,
    )(a0, a1, b0, a2, a3, b1)
    inverse = call(inverse_kernel, "factor_second_half", work, out_shape=small, in_specs=[VMEM], out_specs=VMEM)(state)
    hat, hat_rows = call(
        functools.partial(hat_kernel, devices=devices),
        "left_factor",
        work,
        out_shape=(pltpu.HBM((rank, depth), F32), pltpu.VMEM((depth, 4 * rank), BF16)),
        in_specs=[VMEM] * (1 + UNITS),
        out_specs=(HBM, VMEM),
        scratch_shapes=[pltpu.VMEM((rank, depth), F32), pltpu.SemaphoreType.DMA((UNITS,))],
    )(inverse, a0, a1, b0, a2, a3, b1)

    bits = sorted(bit for bit in walks(devices)[0] if bit >= tensors)
    turns = len(bits) // 2 * 2
    beside = [state, inverse]
    parts = t, None
    for n, bit in enumerate(bits):
        if n:
            t = parts[0] + parts[1]
            if n <= len(beside):
                t, _ = lax.optimization_barrier((t, beside[n - 1]))
        parts = (swap(t, 1), swap(t, 1 ^ bit)) if n < turns else (t, swap(t, bit))

    half = depth // 2
    cuts = [half * n // 18 // 16 * 16 for n in (0, 1, 3, 6, 10, 14, 18)]
    error, q_new = call(
        functools.partial(error_kernel, replicas=replicas, cuts=cuts, devices=devices),
        "new_error",
        work,
        out_shape=(pltpu.HBM((depth, columns), F32), pltpu.HBM((rank, columns), F32)),
        in_specs=[VMEM] * 6,
        out_specs=(HBM, HBM),
        scratch_shapes=[
            pltpu.VMEM((depth, columns), F32),
            pltpu.VMEM((rank, columns), F32),
            pltpu.SemaphoreType.DMA((2 * len(cuts) - 2,)),
            pltpu.SemaphoreType.DMA(()),
        ],
    )(*parts, inverse, hat_rows, m, m2)
    return (error[None], hat.T, q_new.T)


def solution(mesh):
    placed = (P("dp", None, "tensor"), P("dp", None, "tensor"), P("tensor", None))
    return jax.shard_map(
        shards,
        mesh=mesh,
        in_specs=placed,
        out_specs=(P("dp", None, "tensor"), P(), P("tensor", None)),
        check_vma=False,
    )
```

```python
import functools

import jax
import jax.numpy as jnp
from jax import lax
from jax.experimental import pallas as pl
from jax.experimental.pallas import tpu as pltpu
from jax.sharding import PartitionSpec as P

F32, BF16 = jnp.float32, jnp.bfloat16
VMEM = pl.BlockSpec(memory_space=pltpu.VMEM)
HBM = pl.BlockSpec(memory_space=pltpu.HBM)
AXES = ("dp", "tensor")
LIMIT = 12 * 2**20
UNITS = 6
FIRST = 13


def split(x, terms):
    out = []
    for _ in range(terms):
        t = x.astype(BF16)
        out.append(t)
        x = x - t.astype(F32)
    return out


def stack(terms):
    return jnp.concatenate(terms, axis=0)


def dot(a, b, contract):
    return lax.dot_general(a, b, ((contract[:1], contract[1:]), ((), ())), preferred_element_type=F32)


def fold(x, rank):
    return functools.reduce(jnp.add, [x[i : i + rank] for i in range(0, x.shape[0], rank)])


def six_left(x):
    a, b, c = split(x, 3)
    return jnp.concatenate([a, a, b, a, b, c], axis=1)


def six_right(x):
    u, v, w = split(x, 3)
    return stack([u, v, u, w, v, u])


def walks(devices):
    bits = []
    bit = 2
    while bit < devices:
        bits.append(bit)
        bit *= 2
    walk = bits[::2] + bits[1::2]
    return walk, walk[1:] + walk[:1]


def role(place):
    return place.bit_count() & 1


def sides(devices):
    place = lax.axis_index("dp") * lax.axis_size("tensor") + lax.axis_index("tensor")
    half = 0
    for n in range(devices.bit_length() - 1):
        half = half ^ ((place >> n) & 1)
    first, second = ((place >> (walk[0].bit_length() - 1)) & 1 for walk in walks(devices))
    return (1 - half, jnp.where(half == 0, second, first)), (half, jnp.where(half == 0, first, second))


def start(pairs):
    for pair in pairs:
        for copy in pair:
            copy.start()


def wait(pairs):
    for pair in pairs:
        for copy in pair:
            copy.wait()


def left_kernel(q_hbm, g_hbm, e_hbm, m_ref, mh_ref, ml_ref, e_ref, g_ref, send_a, send_b, q_buf, g_buf, q_sem, sems, *, devices):
    theirs, mine = sides(devices)
    half = e_ref.shape[0]
    block = half // 2
    q_copy = pltpu.make_async_copy(q_hbm, q_buf, q_sem)
    q_copy.start()
    copies = []
    for n in range(4):
        source = pl.ds(pl.multiple_of((mine if n > 1 else theirs)[0] * half + n % 2 * block, block), block)
        to = pl.ds(n % 2 * block, block)
        copies.append(
            (
                pltpu.make_async_copy(e_hbm.at[source], (e_ref if n > 1 else m_ref).at[to], sems.at[n, 1]),
                pltpu.make_async_copy(g_hbm.at[source], (g_ref if n > 1 else g_buf).at[to], sems.at[n, 0]),
            )
        )
    start(copies[:3])
    q_copy.wait()
    q = stack(split(q_buf[...], 3))
    for n in range(2):
        wait(copies[n : n + 1])
        if n == 0:
            start(copies[3:])
        at = slice(n * block, (n + 1) * block)
        m = m_ref[at] + g_buf[at].astype(F32)
        m_ref[at] = m
        place(products(q, m, mh_ref, ml_ref, at), n * block, theirs[1], send_a, send_b)
    wait(copies[2:])


def left_rest_kernel(q_ref, e_ref, g_ref, m_ref, mh_ref, ml_ref, keep_a, keep_b, *, devices):
    _, (_, bit) = sides(devices)
    half = e_ref.shape[0]
    block = half // 2
    q = stack(split(q_ref[...], 3))
    for n in range(2):
        at = slice(n * block, (n + 1) * block)
        m = e_ref[at] + g_ref[at].astype(F32)
        m_ref[at] = m
        place(products(q, m, mh_ref, ml_ref, at), n * block, bit, keep_a, keep_b)


def place(p, start, bit, out_a, out_b):
    rows = out_b.shape[1]
    at = 0
    while at < p.shape[1]:
        unit, inside = (start + at) // rows, (start + at) % rows
        width = min(rows - inside, p.shape[1] - at)
        columns = slice(inside, inside + width)
        if unit == 2:
            out_b[:, columns] = p[:, at : at + width]
        else:
            out_a[1 - bit if unit == 0 else bit, :, columns] = p[:, at : at + width]
        at += width


def products(q, m, mh_ref, ml_ref, at):
    mh, ml = split(m, 2)
    mh_ref[at] = mh
    ml_ref[at] = ml
    return fold(dot(q, mh, (1, 1)) + dot(q, ml, (1, 1)), q.shape[0] // 3)


def square(p, rank):
    g = fold(dot(p, p, (1, 1)), rank)
    return g[:, :rank] + g[:, rank : 2 * rank] + g[:, 2 * rank :]


def terms_of(pieces):
    return jnp.concatenate([stack(split(x[...], 3)) for x in pieces], axis=1)


def unit_at(n, rows):
    return pl.ds(n * rows if isinstance(n, int) else pl.multiple_of(n * rows, rows), rows)


def right_early_kernel(a1, b0, a3, b1, a2, mh_ref, ml_ref, mh2_ref, ml2_ref, t_ref, *, devices):
    rank, rows = a1.shape
    (_, their_bit), (_, bit) = sides(devices)
    t = 0.0
    for ref, unit, hs, ls in (
        (a3, bit, mh2_ref, ml2_ref),
        (b1, 2, mh2_ref, ml2_ref),
        (a1, their_bit, mh_ref, ml_ref),
        (b0, 2, mh_ref, ml_ref),
        (a2, 1 - bit, mh2_ref, ml2_ref),
    ):
        at = unit_at(unit, rows)
        p = terms_of((ref,))
        t = t + dot(p, hs[at], (1, 0)) + dot(p, ls[at], (1, 0))
    t_ref[...] = fold(t, rank)


def right_kernel(p_ref, mh_ref, ml_ref, before, t_ref, *, devices):
    rank, rows = p_ref.shape
    p = terms_of((p_ref,))
    at = unit_at(1 - sides(devices)[0][1], rows)
    t_ref[...] = before[...] + fold(dot(p, mh_ref[at], (1, 0)) + dot(p, ml_ref[at], (1, 0)), rank)


def eliminate(a, pivots):
    rank = a.shape[0]
    row = lax.broadcasted_iota(jnp.int32, (rank, 1), 0)
    for k in pivots:
        line = a[k : k + 1, :] / a[k : k + 1, k : k + 1]
        a = a - jnp.where(row > k, a[:, k : k + 1], 0.0) * line
    return a


def factor_kernel(*refs):
    pieces, state_ref = refs[:UNITS], refs[UNITS]
    rank = pieces[0].shape[0]
    gram = square(terms_of(pieces), rank)
    row = lax.broadcasted_iota(jnp.int32, (rank, 128), 0)
    lane = lax.broadcasted_iota(jnp.int32, (rank, 128), 1)
    eye = (lane == row + rank).astype(F32)
    state_ref[...] = eliminate(jnp.concatenate([gram, eye[:, rank:]], axis=1), range(FIRST))


def inverse_kernel(state_ref, inv_ref):
    rank = state_ref.shape[0]
    a = eliminate(state_ref[...], range(FIRST, rank - 1))
    row = lax.broadcasted_iota(jnp.int32, a.shape, 0)
    lane = lax.broadcasted_iota(jnp.int32, a.shape, 1)
    pivots = jnp.sum(jnp.where(row == lane, a, 0.0), axis=1, keepdims=True)
    inv_ref[...] = a[:, rank : 2 * rank] / jnp.sqrt(pivots)


def hat_kernel(inv_ref, *refs, devices):
    pieces, (hat_hbm, rows_ref, hat_buf, sems) = refs[:UNITS], refs[UNITS:]
    rows = pieces[0].shape[1]
    inverse = inv_ref[...]
    left, back = six_left(inverse), six_left(inverse.T)
    copies, units = [], []
    for n, (core, bit) in enumerate(sides(devices)):
        for k, unit in enumerate((1 - bit, bit, 2)):
            i = 3 * n + k
            units.append(3 * n + unit)
            at = pl.ds(i * rows, rows)
            hat_buf[:, at] = dot(left, six_right(pieces[i][...]), (1, 0))
            copies.append(pltpu.make_async_copy(hat_buf.at[:, at], hat_hbm.at[:, unit_at(3 * core + unit, rows)], sems.at[i]))
            copies[-1].start()
    for i in range(UNITS):
        u, v = split(dot(back, six_right(hat_buf[:, i * rows : (i + 1) * rows]), (1, 0)), 2)
        rows_ref[unit_at(units[i], rows), :] = stack([u, v, u, v]).T
    for copy in copies:
        copy.wait()


def error_kernel(t0_ref, t1_ref, inv_ref, rows_ref, m_ref, m2_ref, out_hbm, q_hbm, buf, q_buf, sems, q_sem, *, replicas, cuts, devices):
    t = (t0_ref[...] + t1_ref[...]) / replicas
    u, v = split(t, 2)
    terms = stack([u, u, v, v])
    half = m_ref.shape[0]
    copies = []
    for source, side, shift in ((m_ref, 0, 0), (m2_ref, 1, half)):
        for at, end in zip(cuts[:-1], cuts[1:], strict=True):
            here = slice(shift + at, shift + end)
            buf[here] = source[at:end] - dot(rows_ref[here], terms, (1, 0))
            to = pl.ds(pl.multiple_of(sides(devices)[side][0] * half + at, 16), end - at)
            copies.append(pltpu.make_async_copy(buf.at[pl.ds(shift + at, end - at)], out_hbm.at[to], sems.at[len(copies)]))
            copies[-1].start()
    q_buf[...] = dot(six_left(inv_ref[...]), six_right(t), (1, 0))
    copies.append(pltpu.make_async_copy(q_buf, q_hbm, q_sem))
    copies[-1].start()
    for copy in copies:
        copy.wait()


def shards(gradient, error_buffer, q_given):
    replicas, tensors = lax.axis_size("dp"), lax.axis_size("tensor")
    devices = replicas * tensors
    depth, columns = gradient.shape[1:]
    rank = q_given.shape[1]
    rows = depth // UNITS

    def call(kernel, name, flops, **kw):
        made = pl.pallas_call(
            kernel,
            name=name,
            compiler_params=pltpu.CompilerParams(vmem_limit_bytes=LIMIT),
            cost_estimate=pl.CostEstimate(flops=flops, bytes_accessed=0, transcendentals=0),
            **kw,
        )
        spaces = [pltpu.HBM if spec is HBM else pltpu.VMEM for spec in kw["in_specs"]]
        return lambda *args: made(*(pltpu.with_memory_space_constraint(x, space) for x, space in zip(args, spaces, strict=True)))

    unit = pltpu.VMEM((rank, rows), F32)
    small = pltpu.VMEM((rank, rank), F32)
    wide = pltpu.VMEM((rank, columns), F32)
    work = 6 * depth * columns * rank

    merged = tuple(pltpu.VMEM((depth // 2, columns), kind) for kind in (F32, BF16, BF16))
    two = pltpu.VMEM((2, rank, rows), F32)
    m, mh, ml, e_own, g_own, send_a, send_b = call(
        functools.partial(left_kernel, devices=devices),
        "left_products",
        work,
        out_shape=merged + merged[:2] + (two, unit),
        in_specs=[HBM] * 3,
        out_specs=(VMEM,) * 7,
        scratch_shapes=[
            pltpu.VMEM((rank, columns), F32),
            pltpu.VMEM((depth // 2, columns), BF16),
            pltpu.SemaphoreType.DMA(()),
            pltpu.SemaphoreType.DMA((4, 2)),
        ],
    )(q_given.T, gradient[0], error_buffer[0])
    m2, mh2, ml2, keep_a, keep_b = call(
        functools.partial(left_rest_kernel, devices=devices),
        "left_products_rest",
        work,
        out_shape=merged + (two, unit),
        in_specs=[VMEM] * 3,
        out_specs=(VMEM,) * 5,
    )(q_given.T, e_own, g_own)

    def swap(x, bit):
        return lax.ppermute(x, AXES, [(i, i ^ bit) for i in range(devices)])

    def cross(x, *bits):
        return lax.ppermute(x, AXES, [(i, i ^ 1 ^ bits[role(i)]) for i in range(devices)])

    walk = list(zip(*walks(devices), strict=True))
    both = keep_a + swap(send_a, 1)
    b1 = keep_b + swap(send_b, 1)
    sent, a3 = both[0], both[1]
    for n, bits in enumerate(walk):
        arrived = cross(sent if n == 0 else a3, *bits), cross(b1, *bits)
        a3, b1 = a3 + arrived[0], b1 + arrived[1]
    a2 = cross(a3, *walk[0])
    a1, b0, a0 = swap(a3, 1), swap(b1, 1), swap(a2, 1)

    t = call(
        functools.partial(right_early_kernel, devices=devices),
        "right_products",
        work,
        out_shape=wide,
        in_specs=[VMEM] * 9,
        out_specs=VMEM,
    )(a1, b0, a3, b1, a2, mh, ml, mh2, ml2)
    t = call(
        functools.partial(right_kernel, devices=devices),
        "right_products_last",
        work,
        out_shape=wide,
        in_specs=[VMEM] * 4,
        out_specs=VMEM,
    )(a0, mh, ml, t)

    state = call(
        factor_kernel,
        "factor_first_half",
        work,
        out_shape=pltpu.VMEM((rank, 128), F32),
        in_specs=[VMEM] * UNITS,
        out_specs=VMEM,
    )(a0, a1, b0, a2, a3, b1)
    inverse = call(inverse_kernel, "factor_second_half", work, out_shape=small, in_specs=[VMEM], out_specs=VMEM)(state)
    hat, hat_rows = call(
        functools.partial(hat_kernel, devices=devices),
        "left_factor",
        work,
        out_shape=(pltpu.HBM((rank, depth), F32), pltpu.VMEM((depth, 4 * rank), BF16)),
        in_specs=[VMEM] * (1 + UNITS),
        out_specs=(HBM, VMEM),
        scratch_shapes=[pltpu.VMEM((rank, depth), F32), pltpu.SemaphoreType.DMA((UNITS,))],
    )(inverse, a0, a1, b0, a2, a3, b1)

    bits = sorted(bit for bit in walks(devices)[0] if bit >= tensors)
    turns = len(bits) // 2 * 2
    beside = [state, inverse]
    parts = t, None
    for n, bit in enumerate(bits):
        if n:
            t = parts[0] + parts[1]
            if n <= len(beside):
                t, _ = lax.optimization_barrier((t, beside[n - 1]))
        parts = (swap(t, 1), swap(t, 1 ^ bit)) if n < turns else (t, swap(t, bit))

    half = depth // 2
    cuts = [half * n // 18 // 16 * 16 for n in (0, 1, 5, 10, 18)]
    error, q_new = call(
        functools.partial(error_kernel, replicas=replicas, cuts=cuts, devices=devices),
        "new_error",
        work,
        out_shape=(pltpu.HBM((depth, columns), F32), pltpu.HBM((rank, columns), F32)),
        in_specs=[VMEM] * 6,
        out_specs=(HBM, HBM),
        scratch_shapes=[
            pltpu.VMEM((depth, columns), F32),
            pltpu.VMEM((rank, columns), F32),
            pltpu.SemaphoreType.DMA((2 * len(cuts) - 2,)),
            pltpu.SemaphoreType.DMA(()),
        ],
    )(*parts, inverse, hat_rows, m, m2)
    return (error[None], hat.T, q_new.T)


def solution(mesh):
    placed = (P("dp", None, "tensor"), P("dp", None, "tensor"), P("tensor", None))
    return jax.shard_map(
        shards,
        mesh=mesh,
        in_specs=placed,
        out_specs=(P("dp", None, "tensor"), P(), P("tensor", None)),
        check_vma=False,
    )
```
